256 devices in a mesh: row: 16 (over z, y_lo), col: 16 (over x, y_hi, core).
Axes of the slice: x: 4, y: 4 (y_hi: 2, y_lo: 2; y = y_hi * 2 + y_lo), z: 8, core: 2. Of those that a mesh axis runs over, the one named last changes fastest.
Arguments:
- memory: bfloat16 [8192, 4096], P('row', 'col'), may hold values from -0.09375 to 0.09375
- joined_weight: bfloat16 [2, 4096, 8192], P(None, 'row', 'col'), may hold values from -0.09375 to 0.09375
- joined_cotangent: bfloat16 [2, 8192, 8192], P(None, 'row', 'col'), may hold values from -6 to 6
Outputs:
- memory_grad: bfloat16 [8192, 4096], P('row', 'col')
- weight_grad: float32 [2, 4096, 8192], P(None, 'row', 'col')
The draws below stay inside these ranges and needn't reach their ends.
All inputs are finite; a program needn't handle non-finite values.
Results may differ from the reference program's by a relative error of at most 0.001.
Values may be sent and summed in bfloat16 or wider, within the bound.
A program may use at most 128 MiB of HBM per device.

```python
import jax
import jax.numpy as jnp
from jax import lax

D = 4096
KV = 8192
LAYERS = 2
ROWS = 8192


def with_spikes(values, stream_key, source, target, shards_of, factor):
    owner, partner = [(jnp.arange(values.shape[dim]) // (values.shape[dim] // shards_of)).reshape([-1 if axis == dim else 1 for axis in range(values.ndim)]) for dim in (source, target)]
    chosen = jax.random.permutation(stream_key, shards_of)[partner]
    strong = (owner == chosen) | (owner == (partner + shards_of // 2) % shards_of)
    return jnp.where(strong, factor * values, values)


def level_of(key, shape, split, low, top_value):
    level, own = 1.0, jax.random.fold_in(key, 6)
    for dim, blocks in split:
        draws = jnp.exp(jax.random.uniform(jax.random.fold_in(own, dim), (blocks,), jnp.float32, low / len(split), top_value / len(split)))
        level = level * jnp.repeat(draws, shape[dim] // blocks).reshape([-1 if axis == dim else 1 for axis in range(len(shape))])
    return level


def scatter_about(own_key, dims, deviation, limit, cuts=(), dtype=jnp.bfloat16):
    entries = jax.random.normal(own_key, dims, jnp.float32) * deviation
    if len(cuts) > 0:
        entries = level_of(own_key, dims, cuts, -0.22, 0.18) * entries
    return jnp.clip(entries, min=-limit, max=limit).astype(dtype)


def heavy_noise(stream_key, dims, spread, bound, cuts, heavy, dtype=jnp.bfloat16):
    drawn = spread * jax.random.normal(stream_key, dims, jnp.float32)
    if cuts:
        drawn = drawn * level_of(stream_key, dims, cuts, -0.22, 0.18)
    return jnp.clip(with_spikes(drawn, jax.random.fold_in(stream_key, 3), *heavy), -bound, bound).astype(dtype)


def setup_inputs(seed: int = 0) -> dict:
    key_of = jax.random.split(jax.random.key(seed), 4)
    memory = heavy_noise(key_of[0], (ROWS, D), (ROWS ** -0.5), 0.09375, ((0, 16), (1, 16)), (0, 1, 16, 2.0))
    joined_weight = heavy_noise(key_of[1], (LAYERS, D, KV), KV ** -0.5, 0.09375, ((1, 16), (2, 16)), (2, 1, 16, 2.0))
    joined_cotangent = scatter_about(key_of[2], (LAYERS, ROWS, KV), 1.0, 6.0, ((1, 16), (2, 16)))
    return {"memory": memory, "joined_weight": joined_weight, "joined_cotangent": joined_cotangent}


def reference(memory, joined_weight, joined_cotangent):
    memory_total = jnp.zeros((memory.shape[0], memory.shape[1]), jnp.float32)
    grads = []
    for layer_index in range(LAYERS):
        cotangent = joined_cotangent[layer_index]
        weight = joined_weight[layer_index]
        memory_total = memory_total + lax.dot_general(cotangent, weight, (((1,), (1,)), ((), ())), preferred_element_type=jnp.float32)
        grads.append(lax.dot_general(memory, cotangent, (((0,), (0,)), ((), ())), preferred_element_type=jnp.float32))
    return memory_total.astype(jnp.bfloat16), jnp.stack(grads)
```

```python
import jax
import jax.numpy as jnp
from jax import lax
from jax.experimental import pallas as pl
from jax.experimental.pallas import tpu as pltpu
from jax.sharding import PartitionSpec as P

MESH = pl.DeviceIdType.MESH
F32 = jnp.float32
ORDER = (0, 7, 1, 6, 2, 5, 3, 4)


def dot_nt(a, b):
    return lax.dot_general(a, b, (((1,), (1,)), ((), ())), preferred_element_type=F32)


def dot_tn(a, b):
    return lax.dot_general(a, b, (((0,), (0,)), ((), ())), preferred_element_type=F32)


def kernel(
    m_ref, w_ref, c_ref, mg_ref, wg_ref,
    c_all, w_all, m_all, p_own, p_send, p_recv, x_recv, s_own, y_recv, o_send, acc, wg_recv,
    c_ss, c_rs, w_ss, w_rs, m1_ss, m1_rs, m2_ss, m2_rs, m3_ss, p_ss, p_rs, x_ss, x_rs, y_ss, y_rs,
    o_ss, o_rs, g_ss, g_rs,
):
    row, col = lax.axis_index("row"), lax.axis_index("col")
    z, b = lax.div(row, 2), lax.rem(row, 2)
    k, core = lax.div(col, 2), lax.rem(col, 2)
    x, h = lax.div(k, 2), lax.rem(k, 2)
    up = (lax.rem(z + 1, 8) * 2 + b, col)
    down = (lax.rem(z + 7, 8) * 2 + b, col)
    y_pair = (z * 2 + 1 - b, col)
    core_pair = (row, k * 2 + 1 - core)
    h_pair = (row, (x * 2 + 1 - h) * 2 + core)
    xs = [lax.rem(x + o, 4) for o in range(4)]
    x_peer = [(row, (xs[o] * 2 + h) * 2 + core) for o in range(4)]
    ks = [lax.rem(k + o, 8) for o in range(8)]
    zs = [lax.rem(z + o, 8) for o in range(8)]
    plane_peer = [(k * 2 + b, ks[o] * 2 + core) for o in range(8)]
    line_peer = [(zs[o] * 2 + b, z * 2 + core) for o in range(8)]
    diagonal = z == k

    barrier = pltpu.get_barrier_semaphore()
    greeted = [up, down, y_pair, core_pair, h_pair] + x_peer[1:] + plane_peer + line_peer
    for peer in greeted:
        pl.semaphore_signal(barrier, inc=1, device_id=peer, device_id_type=MESH)
    pl.semaphore_wait(barrier, len(greeted))

    sent = []

    def send(src, dst, ss, rs, peer):
        copy = pltpu.make_async_remote_copy(
            src_ref=src, dst_ref=dst, send_sem=ss, recv_sem=rs, device_id=peer, device_id_type=MESH
        )
        copy.start()
        sent.append(copy)

    def arrived(dst, rs):
        pltpu.make_async_copy(dst, dst, rs).wait()

    slot = lax.rem(z - k + 8, 8)
    m1 = []
    for o in range(8):
        src = m_ref.at[pl.ds(pl.multiple_of(ks[o] * 64, 64), 64), :]
        dst = m_all.at[core, ks[o], slot]
        copy = pltpu.make_async_remote_copy(
            src_ref=src, dst_ref=dst, send_sem=m1_ss.at[o], recv_sem=m1_rs.at[slot],
            device_id=plane_peer[o], device_id_type=MESH,
        )
        if o == 0:
            own = pltpu.make_async_copy(src, dst, m1_rs.at[slot])
            pl.when(diagonal)(own.start)
            pl.when(jnp.logical_not(diagonal))(copy.start)
        else:
            copy.start()
        m1.append(copy)

    send(w_ref, w_all.at[b], w_ss, w_rs, y_pair)

    def c_src(offset, l):
        return c_ref.at[l] if offset == 0 else c_all.at[offset, l]

    def c_step(step, l):
        if step < 4 or l == 0:
            src = (8 - (step - 1)) % 8
            send(c_src(src, l), c_all.at[8 - step, l], c_ss.at[0, step - 1, l], c_rs.at[0, step - 1, l], up)
        if step < 4 or l == 1:
            send(c_src(step - 1, l), c_all.at[step, l], c_ss.at[1, step - 1, l], c_rs.at[1, step - 1, l], down)

    def c_wait(step, l):
        if step < 4 or l == 0:
            arrived(c_all.at[8 - step, l], c_rs.at[0, step - 1, l])
        if step < 4 or l == 1:
            arrived(c_all.at[step, l], c_rs.at[1, step - 1, l])

    c_step(1, 0)
    c_step(1, 1)
    w_all[b] = w_ref[...]

    for o in range(8):
        arrived(m_all.at[core, k, o], m1_rs.at[o])
    kh = x * 2 + 1 - h

    def share(piece, ss, to_h):
        ref = m_all.at[core, piece]
        if to_h:
            send(ref, ref, m2_ss.at[ss], m2_rs.at[core, piece], h_pair)
        for o in (1, 3, 2):
            send(ref, ref, m2_ss.at[ss + o], m2_rs.at[core, piece], x_peer[o])

    def to_core(piece, ss):
        ref = m_all.at[core, piece]
        send(ref, ref, m3_ss.at[ss], m2_rs.at[core, piece], core_pair)

    share(k, 0, True)
    to_core(k, 0)

    arrived(w_all.at[1 - b], w_rs)

    def stage_a(offset):
        for side, dst in ((1 - core, p_send), (core, p_own)):

            @pl.loop(0, 2)
            def _(t):
                rows = pl.ds(pl.multiple_of(t * 256, 256), 256)
                total = dot_nt(c_src(offset, 0)[rows, :], w_all[side, 0])
                total += dot_nt(c_src(offset, 1)[rows, :], w_all[side, 1])
                dst[offset, rows, :] = total

            if dst is p_send:
                send(p_send.at[offset], p_recv.at[offset], p_ss.at[offset], p_rs.at[offset], core_pair)

    def stage_b(offset):
        arrived(p_recv.at[offset], p_rs.at[offset])
        p_own[offset] += p_recv[offset]
        for o in (2, 1, 3):
            rows = pl.ds(pl.multiple_of(xs[o] * 128, 128), 128)
            send(
                p_own.at[offset, rows, :], x_recv.at[offset, o - 1],
                x_ss.at[offset, o - 1], x_rs.at[offset, o - 1], x_peer[o],
            )

    def stage_c(offset):
        for o in (1, 3, 2):
            arrived(x_recv.at[offset, o - 1], x_rs.at[offset, o - 1])
        total = p_own[offset, pl.ds(pl.multiple_of(x * 128, 128), 128), :]
        for o in (1, 3, 2):
            total += x_recv[offset, o - 1]
        s_own[offset] = total
        half = pl.ds(pl.multiple_of((1 - h) * 64, 64), 64)
        send(s_own.at[offset, half, :], y_recv.at[offset], y_ss.at[offset], y_rs.at[offset], h_pair)

    finals = []

    def stage_d(offset):
        arrived(y_recv.at[offset], y_rs.at[offset])
        total = s_own[offset, pl.ds(pl.multiple_of(h * 64, 64), 64), :] + y_recv[offset]
        o_send[offset] = total.astype(jnp.bfloat16)
        copy = pltpu.make_async_remote_copy(
            src_ref=o_send.at[offset], dst_ref=mg_ref.at[k], send_sem=o_ss.at[offset], recv_sem=o_rs.at[k],
            device_id=line_peer[offset], device_id_type=MESH,
        )
        if offset == 0:
            own = pltpu.make_async_copy(o_send.at[0], mg_ref.at[k], o_rs.at[k])
            pl.when(diagonal)(own.start)
            pl.when(jnp.logical_not(diagonal))(copy.start)
        else:
            copy.start()
        finals.append(copy)

    def weight(offset, first):
        for side in range(2):
            m_t = m_all[side, :, offset].reshape(512, 256).T
            for l in range(2):
                term = jnp.dot(m_t, c_src(offset, l)[...], preferred_element_type=F32)
                if first:
                    acc[l, side] = term
                else:
                    acc[l, side] += term

    stage_a(0)
    c_wait(1, 0)
    c_step(2, 0)
    arrived(m_all.at[core, kh], m2_rs.at[core, kh])
    share(kh, 4, False)
    to_core(kh, 1)
    stage_b(0)
    c_wait(1, 1)
    c_step(2, 1)
    stage_a(7)
    stage_a(1)
    stage_c(0)
    stage_b(7)
    stage_b(1)
    c_wait(2, 0)
    c_step(3, 0)
    n = 2
    for o in (1, 3, 2):
        for t in range(2):
            piece = xs[o] * 2 + t
            arrived(m_all.at[core, piece], m2_rs.at[core, piece])
            to_core(piece, n)
            n += 1
    stage_d(0)
    stage_c(7)
    stage_c(1)
    c_wait(2, 1)
    c_step(3, 1)
    stage_a(6)
    stage_a(2)
    stage_d(7)
    stage_d(1)
    for t in range(8):
        arrived(m_all.at[1 - core, t], m2_rs.at[1 - core, t])
    weight(0, True)
    stage_b(6)
    stage_b(2)
    c_wait(3, 0)
    c_step(4, 0)
    weight(7, False)
    stage_c(6)
    stage_c(2)
    weight(1, False)
    c_wait(3, 1)
    c_step(4, 1)
    stage_a(5)
    stage_a(3)
    weight(6, False)
    stage_b(5)
    stage_b(3)
    stage_d(6)
    stage_d(2)
    weight(2, False)
    weight(5, False)
    weight(3, False)
    c_wait(4, 0)
    c_wait(4, 1)
    stage_a(4)
    weight(4, False)
    for l in range(2):
        send(acc.at[l, 1 - b], wg_recv.at[l], g_ss.at[l], g_rs.at[l], y_pair)
    stage_b(4)
    stage_c(5)
    stage_c(3)
    stage_d(5)
    stage_d(3)
    stage_c(4)
    stage_d(4)
    for l in range(2):
        arrived(wg_recv.at[l], g_rs.at[l])
        wg_ref[l] = acc[l, b] + wg_recv[l]
    for t in range(8):
        arrived(mg_ref.at[t], o_rs.at[t])

    for copy in sent:
        copy.wait_send()
    for copies in (m1, finals):
        pl.when(jnp.logical_not(diagonal))(copies[0].wait_send)
        for copy in copies[1:]:
            copy.wait_send()


def on_device(memory, joined_weight, joined_cotangent):
    dma = pltpu.SemaphoreType.DMA
    bf16 = jnp.bfloat16
    memory_grad, weight_grad = pl.pallas_call(
        kernel,
        out_shape=(
            jax.ShapeDtypeStruct((8, 64, 256), bf16),
            jax.ShapeDtypeStruct((2, 256, 512), F32),
        ),
        in_specs=[pl.BlockSpec(memory_space=pltpu.VMEM)] * 3,
        out_specs=(pl.BlockSpec(memory_space=pltpu.VMEM),) * 2,
        scratch_shapes=[
            pltpu.VMEM((8, 2, 512, 512), bf16),
            pltpu.VMEM((2, 2, 256, 512), bf16),
            pltpu.VMEM((2, 8, 8, 64, 256), bf16),
            pltpu.VMEM((8, 512, 256), F32),
            pltpu.VMEM((8, 512, 256), F32),
            pltpu.VMEM((8, 512, 256), F32),
            pltpu.VMEM((8, 3, 128, 256), F32),
            pltpu.VMEM((8, 128, 256), F32),
            pltpu.VMEM((8, 64, 256), F32),
            pltpu.VMEM((8, 64, 256), bf16),
            pltpu.VMEM((2, 2, 256, 512), F32),
            pltpu.VMEM((2, 256, 512), F32),
            dma((2, 4, 2)), dma((2, 4, 2)),
            dma, dma,
            dma((8,)), dma((8,)),
            dma((8,)), dma((2, 8)), dma((8,)),
            dma((8,)), dma((8,)),
            dma((8, 3)), dma((8, 3)),
            dma((8,)), dma((8,)),
            dma((8,)), dma((8,)),
            dma((2,)), dma((2,)),
        ],
        compiler_params=pltpu.CompilerParams(
            collective_id=0, has_side_effects=True, vmem_limit_bytes=52 * 1024 * 1024
        ),
    )(memory, joined_weight, joined_cotangent)
    return memory_grad.reshape(512, 256), weight_grad


def solution(mesh):
    in_specs = (P("row", "col"), P(None, "row", "col"), P(None, "row", "col"))
    out_specs = (P("row", "col"), P(None, "row", "col"))
    return jax.shard_map(
        on_device, mesh=mesh, in_specs=in_specs, out_specs=out_specs, check_vma=False
    )
```

```python
import jax
import jax.numpy as jnp
from jax import lax
from jax.experimental import pallas as pl
from jax.experimental.pallas import tpu as pltpu
from jax.sharding import PartitionSpec as P

MESH = pl.DeviceIdType.MESH
F32 = jnp.float32
H_FIRST = (1, 2, 3)


def dot_nt(a, b):
    return lax.dot_general(a, b, (((1,), (1,)), ((), ())), preferred_element_type=F32)


def kernel(
    m_ref, w_ref, c_ref, mg_ref, wg_ref,
    c_all, w_all, m_a, m_all, p_own, p_send, p_recv, x_recv, s_own, y_recv, h_recv, h_own, v_recv,
    o_send, acc, wg_recv,
    in_s, c_ss, c_rs, w_ss, w_rs, ma_ss, ma_rs, mb_ss, mb_rs, m2_ss, m2_rs, m3_ss, p_ss, p_rs,
    x_ss, x_rs, y_ss, y_rs, h_ss, h_rs, v_ss, v_rs, o_ss, o_rs, g_ss, g_rs,
):
    row, col = lax.axis_index("row"), lax.axis_index("col")
    z, b = lax.div(row, 2), lax.rem(row, 2)
    k, core = lax.div(col, 2), lax.rem(col, 2)
    x, h = lax.div(k, 2), lax.rem(k, 2)
    ks = [lax.rem(k + o, 8) for o in range(8)]
    zs = [lax.rem(z + o, 8) for o in range(8)]
    xs = [lax.rem(x + o, 4) for o in range(4)]
    plane = [(row, ks[o] * 2 + core) for o in range(8)]
    line = [(zs[o] * 2 + b, col) for o in range(8)]
    up, down = line[1], line[7]
    y_pair = (z * 2 + 1 - b, col)
    core_pair = (row, k * 2 + 1 - core)
    h_pair = (row, (x * 2 + 1 - h) * 2 + core)
    x_peer = [(row, (xs[o] * 2 + h) * 2 + core) for o in range(4)]
    home = [(zs[o] * 2 + b, z * 2 + core) for o in range(8)]
    at_home = z == k

    c_in = pltpu.make_async_copy(c_ref, c_all.at[0], in_s.at[0])
    w_in = pltpu.make_async_copy(w_ref, w_all.at[b], in_s.at[1])
    c_in.start()
    w_in.start()

    barrier = pltpu.get_barrier_semaphore()
    greeted = plane[1:] + line[1:] + [y_pair, core_pair]
    for peer in greeted:
        pl.semaphore_signal(barrier, inc=1, device_id=peer, device_id_type=MESH)
    pl.semaphore_wait(barrier, len(greeted))

    sent = []

    def send(src, dst, ss, rs, peer):
        copy = pltpu.make_async_remote_copy(
            src_ref=src, dst_ref=dst, send_sem=ss, recv_sem=rs, device_id=peer, device_id_type=MESH
        )
        copy.start()
        sent.append(copy)

    def arrived(dst, rs):
        pltpu.make_async_copy(dst, dst, rs).wait()

    def part(offset, l, r):
        return c_all.at[offset, l, pl.ds(r * 256, 256), :]

    def c_step(step, l, r):
        mine = c_ref.at[l, pl.ds(r * 256, 256), :]
        if step < 4 or r == 0:
            src = mine if step == 1 else part(9 - step, l, r)
            send(src, part(8 - step, l, r), c_ss.at[0, step - 1, l, r], c_rs.at[0, step - 1, l, r], up)
        if step < 4 or r == 1:
            src = mine if step == 1 else part(step - 1, l, r)
            send(src, part(step, l, r), c_ss.at[1, step - 1, l, r], c_rs.at[1, step - 1, l, r], down)

    def c_wait(step, l, r):
        if step < 4 or r == 0:
            arrived(part(8 - step, l, r), c_rs.at[0, step - 1, l, r])
        if step < 4 or r == 1:
            arrived(part(step, l, r), c_rs.at[1, step - 1, l, r])

    def c_next(step, l):
        for r in range(2):
            c_wait(step, l, r)
            if step < 4:
                c_step(step + 1, l, r)

    c_step(1, 0, 0)
    c_step(1, 0, 1)

    def m_rows(j):
        return m_ref.at[pl.ds(pl.multiple_of(j * 64, 64), 64), :]

    for o in range(1, 8):
        send(m_rows(ks[o]), m_a.at[k], ma_ss.at[o], ma_rs.at[k], plane[o])
    m_in = pltpu.make_async_copy(m_rows(k), m_a.at[k], ma_rs.at[k])
    m_in.start()
    send(w_ref, w_all.at[b], w_ss, w_rs, y_pair)

    for o in (4, 3, 5, 2, 6, 1, 7, 0):
        piece = m_a.at[zs[o]]
        arrived(piece, ma_rs.at[zs[o]])
        slot = (8 - o) % 8
        if o:
            send(piece, m_all.at[core, k, slot], mb_ss.at[o], mb_rs.at[slot], line[o])
        else:
            pltpu.make_async_copy(piece, m_all.at[core, k, 0], mb_rs.at[0]).start()

    kh = x * 2 + 1 - h

    def share(piece, n, to_h):
        ref = m_all.at[core, piece]
        if to_h:
            send(ref, ref, m2_ss.at[n], m2_rs.at[core, piece], h_pair)
        for o in (1, 3, 2):
            send(ref, ref, m2_ss.at[n + o], m2_rs.at[core, piece], x_peer[o])

    def to_core(piece, n):
        ref = m_all.at[core, piece]
        send(ref, ref, m3_ss.at[n], m2_rs.at[core, piece], core_pair)

    def got(side, piece):
        arrived(m_all.at[side, piece], m2_rs.at[side, piece])

    def partial(offset):
        for side, dst in ((1 - core, p_send), (core, p_own)):

            @pl.loop(0, 2)
            def _(t):
                rows = pl.ds(pl.multiple_of(t * 256, 256), 256)
                total = dot_nt(c_all[offset, 0, rows, :], w_all[side, 0])
                total += dot_nt(c_all[offset, 1, rows, :], w_all[side, 1])
                dst[offset, pl.ds(t * 2, 2)] = total.reshape(2, 2, 64, 256)

            if dst is p_send:
                send(p_send.at[offset], p_recv.at[offset], p_ss.at[offset], p_rs.at[offset], core_pair)

    def scatter(offset):
        arrived(p_recv.at[offset], p_rs.at[offset])
        p_own[offset] += p_recv[offset]
        if offset in H_FIRST:
            n = H_FIRST.index(offset)
            send(p_own.at[offset, :, 1 - h], h_recv.at[n], h_ss.at[n], h_rs.at[n], h_pair)
            return
        for o in (2, 1, 3):
            send(
                p_own.at[offset, xs[o]], x_recv.at[offset, o - 1],
                x_ss.at[offset, o - 1], x_rs.at[offset, o - 1], x_peer[o],
            )

    def scatter_more(offset):
        if offset in H_FIRST:
            n = H_FIRST.index(offset)
            arrived(h_recv.at[n], h_rs.at[n])
            h_own[n] = p_own[offset, :, h] + h_recv[n]
            for o in (2, 1, 3):
                send(
                    h_own.at[n, xs[o]], v_recv.at[n, o - 1],
                    v_ss.at[n, o - 1], v_rs.at[n, o - 1], x_peer[o],
                )
            return
        for o in (1, 3, 2):
            arrived(x_recv.at[offset, o - 1], x_rs.at[offset, o - 1])
        total = p_own[offset, x]
        for o in (1, 3, 2):
            total += x_recv[offset, o - 1]
        s_own[offset] = total
        send(s_own.at[offset, 1 - h], y_recv.at[offset], y_ss.at[offset], y_rs.at[offset], h_pair)

    def finish(offset):
        if offset in H_FIRST:
            n = H_FIRST.index(offset)
            for o in (1, 3, 2):
                arrived(v_recv.at[n, o - 1], v_rs.at[n, o - 1])
            total = h_own[n, x]
            for o in (1, 3, 2):
                total += v_recv[n, o - 1]
        else:
            arrived(y_recv.at[offset], y_rs.at[offset])
            total = s_own[offset, h] + y_recv[offset]
        o_send[offset] = total.astype(jnp.bfloat16)

    finals = {}

    def deliver(offset):
        copy = pltpu.make_async_remote_copy(
            src_ref=o_send.at[offset], dst_ref=mg_ref.at[k], send_sem=o_ss.at[offset], recv_sem=o_rs.at[k],
            device_id=home[offset], device_id_type=MESH,
        )
        if offset == 0:
            own = pltpu.make_async_copy(o_send.at[0], mg_ref.at[k], o_rs.at[k])
            pl.when(at_home)(own.start)
            pl.when(jnp.logical_not(at_home))(copy.start)
        else:
            copy.start()
        finals[offset] = copy

    def weight(l, side, offset):
        m_t = m_all[side, :, offset].reshape(512, 256).T
        term = jnp.dot(m_t, c_all[offset, l], preferred_element_type=F32)
        if offset == 0:
            acc[l, side] = term
        else:
            acc[l, side] += term

    def weight_send(l):
        send(acc.at[l, 1 - b], wg_recv.at[l], g_ss.at[l], g_rs.at[l], y_pair)

    def weight_end(l):
        arrived(wg_recv.at[l], g_rs.at[l])
        wg_ref[l] = acc[l, b] + wg_recv[l]

    w_in.wait()
    c_in.wait()
    arrived(w_all.at[1 - b], w_rs)
    partial(0)
    c_next(1, 0)
    for o in range(8):
        arrived(m_all.at[core, k, o], mb_rs.at[o])
    share(k, 0, True)
    to_core(k, 0)
    scatter(0)
    got(core, kh)
    share(kh, 4, False)
    to_core(kh, 1)
    c_next(2, 0)
    scatter_more(0)
    c_next(3, 0)
    c_step(1, 1, 0)
    c_step(1, 1, 1)
    n = 2
    for o in (1, 3, 2):
        for t in range(2):
            got(core, xs[o] * 2 + t)
            to_core(xs[o] * 2 + t, n)
            n += 1
    finish(0)
    c_next(4, 0)
    for t in range(8):
        got(1 - core, t)
    for side in (1 - b, b):
        for o in range(8):
            weight(0, side, o)
        if side is not b:
            weight_send(0)
    c_next(1, 1)
    partial(7)
    partial(1)
    for o in (0, 7, 1):
        for side in range(2):
            weight(1, side, o)
    scatter(7)
    scatter(1)
    c_next(2, 1)
    partial(6)
    partial(2)
    scatter_more(7)
    scatter_more(1)
    scatter(6)
    scatter(2)
    for o in (6, 2):
        for side in range(2):
            weight(1, side, o)
    weight_end(0)
    c_next(3, 1)
    partial(5)
    partial(3)
    finish(7)
    finish(1)
    scatter_more(6)
    scatter_more(2)
    scatter(5)
    scatter(3)
    for o in (5, 3):
        for side in range(2):
            weight(1, side, o)
    c_next(4, 1)
    weight(1, 1 - b, 4)
    weight_send(1)
    for o in (0, 7, 1):
        deliver(o)
    partial(4)
    scatter(4)
    finish(6)
    finish(2)
    deliver(6)
    deliver(2)
    weight(1, b, 4)
    scatter_more(5)
    scatter_more(3)
    scatter_more(4)
    for o in (5, 3, 4):
        finish(o)
        deliver(o)
    weight_end(1)
    for t in range(8):
        arrived(mg_ref.at[t], o_rs.at[t])

    for copy in sent:
        copy.wait_send()
    pl.when(jnp.logical_not(at_home))(finals[0].wait_send)
    for o in range(1, 8):
        finals[o].wait_send()


def on_device(memory, joined_weight, joined_cotangent):
    dma = pltpu.SemaphoreType.DMA
    bf16 = jnp.bfloat16
    memory_grad, weight_grad = pl.pallas_call(
        kernel,
        out_shape=(
            jax.ShapeDtypeStruct((8, 64, 256), bf16),
            jax.ShapeDtypeStruct((2, 256, 512), F32),
        ),
        in_specs=[pl.BlockSpec(memory_space=pltpu.HBM)] * 3,
        out_specs=(pl.BlockSpec(memory_space=pltpu.VMEM),) * 2,
        scratch_shapes=[
            pltpu.VMEM((8, 2, 512, 512), bf16),
            pltpu.VMEM((2, 2, 256, 512), bf16),
            pltpu.VMEM((8, 64, 256), bf16),
            pltpu.VMEM((2, 8, 8, 64, 256), bf16),
            pltpu.VMEM((8, 4, 2, 64, 256), F32),
            pltpu.VMEM((8, 4, 2, 64, 256), F32),
            pltpu.VMEM((8, 4, 2, 64, 256), F32),
            pltpu.VMEM((8, 3, 2, 64, 256), F32),
            pltpu.VMEM((8, 2, 64, 256), F32),
            pltpu.VMEM((8, 64, 256), F32),
            pltpu.VMEM((3, 4, 64, 256), F32),
            pltpu.VMEM((3, 4, 64, 256), F32),
            pltpu.VMEM((3, 3, 64, 256), F32),
            pltpu.VMEM((8, 64, 256), bf16),
            pltpu.VMEM((2, 2, 256, 512), F32),
            pltpu.VMEM((2, 256, 512), F32),
            dma((2,)),
            dma((2, 4, 2, 2)), dma((2, 4, 2, 2)),
            dma, dma,
            dma((8,)), dma((8,)),
            dma((8,)), dma((8,)),
            dma((8,)), dma((2, 8)), dma((8,)),
            dma((8,)), dma((8,)),
            dma((8, 3)), dma((8, 3)),
            dma((8,)), dma((8,)),
            dma((3,)), dma((3,)),
            dma((3, 3)), dma((3, 3)),
            dma((8,)), dma((8,)),
            dma((2,)), dma((2,)),
        ],
        compiler_params=pltpu.CompilerParams(
            collective_id=0, has_side_effects=True, vmem_limit_bytes=56 * 1024 * 1024
        ),
    )(memory, joined_weight, joined_cotangent)
    return memory_grad.reshape(512, 256), weight_grad


def solution(mesh):
    in_specs = (P("row", "col"), P(None, "row", "col"), P(None, "row", "col"))
    out_specs = (P("row", "col"), P(None, "row", "col"))
    return jax.shard_map(
        on_device, mesh=mesh, in_specs=in_specs, out_specs=out_specs, check_vma=False
    )
```

```python
import jax
import jax.numpy as jnp
from jax import lax
from jax.experimental import pallas as pl
from jax.experimental.pallas import tpu as pltpu
from jax.sharding import PartitionSpec as P

MESH = pl.DeviceIdType.MESH
F32 = jnp.float32
H_FIRST = (1, 2, 3)


def dot_nt(a, b):
    return lax.dot_general(a, b, (((1,), (1,)), ((), ())), preferred_element_type=F32)


def kernel(
    m_ref, w_ref, c_ref, mg_ref, wg_ref,
    c_all, w_all, m_a, m_all, p_own, p_send, p_recv, x_recv, s_own, y_recv, h_recv, h_own, v_recv,
    o_send, acc, wg_recv,
    in_s, c_ss, c_rs, w_ss, w_rs, ma_ss, ma_rs, mb_ss, mb_rs, m2_ss, m2_rs, m3_ss, p_ss, p_rs,
    x_ss, x_rs, y_ss, y_rs, h_ss, h_rs, v_ss, v_rs, o_ss, o_rs, g_ss, g_rs,
):
    row, col = lax.axis_index("row"), lax.axis_index("col")
    z, b = lax.div(row, 2), lax.rem(row, 2)
    k, core = lax.div(col, 2), lax.rem(col, 2)
    x, h = lax.div(k, 2), lax.rem(k, 2)
    ks = [lax.rem(k + o, 8) for o in range(8)]
    zs = [lax.rem(z + o, 8) for o in range(8)]
    xs = [lax.rem(x + o, 4) for o in range(4)]
    plane = [(row, ks[o] * 2 + core) for o in range(8)]
    line = [(zs[o] * 2 + b, col) for o in range(8)]
    up, down = line[1], line[7]
    y_pair = (z * 2 + 1 - b, col)
    core_pair = (row, k * 2 + 1 - core)
    h_pair = (row, (x * 2 + 1 - h) * 2 + core)
    x_peer = [(row, (xs[o] * 2 + h) * 2 + core) for o in range(4)]
    home = [(zs[o] * 2 + b, z * 2 + core) for o in range(8)]
    at_home = z == k

    c_in = pltpu.make_async_copy(c_ref, c_all.at[0], in_s.at[0])
    w_in = pltpu.make_async_copy(w_ref, w_all.at[b], in_s.at[1])
    c_in.start()
    w_in.start()

    barrier = pltpu.get_barrier_semaphore()
    greeted = plane[1:] + line[1:] + [y_pair, core_pair]
    for peer in greeted:
        pl.semaphore_signal(barrier, inc=1, device_id=peer, device_id_type=MESH)
    pl.semaphore_wait(barrier, len(greeted))

    sent = []

    def send(src, dst, ss, rs, peer):
        copy = pltpu.make_async_remote_copy(
            src_ref=src, dst_ref=dst, send_sem=ss, recv_sem=rs, device_id=peer, device_id_type=MESH
        )
        copy.start()
        sent.append(copy)

    def arrived(dst, rs):
        pltpu.make_async_copy(dst, dst, rs).wait()

    def part(offset, l, r):
        return c_all.at[offset, l, pl.ds(r * 256, 256), :]

    def c_step(step, l, r):
        mine = c_ref.at[l, pl.ds(r * 256, 256), :]
        if step < 4 or r == 0:
            src = mine if step == 1 else part(9 - step, l, r)
            send(src, part(8 - step, l, r), c_ss.at[0, step - 1, l, r], c_rs.at[0, step - 1, l, r], up)
        if step < 4 or r == 1:
            src = mine if step == 1 else part(step - 1, l, r)
            send(src, part(step, l, r), c_ss.at[1, step - 1, l, r], c_rs.at[1, step - 1, l, r], down)

    def c_wait(step, l, r):
        if step < 4 or r == 0:
            arrived(part(8 - step, l, r), c_rs.at[0, step - 1, l, r])
        if step < 4 or r == 1:
            arrived(part(step, l, r), c_rs.at[1, step - 1, l, r])

    def c_next(step, l, onward=True):
        for r in range(2):
            c_wait(step, l, r)
            if step < 4 and onward:
                c_step(step + 1, l, r)

    c_step(1, 0, 0)

    def m_rows(j):
        return m_ref.at[pl.ds(pl.multiple_of(j * 64, 64), 64), :]

    for o in range(1, 8):
        send(m_rows(ks[o]), m_a.at[k], ma_ss.at[o], ma_rs.at[k], plane[o])
    m_in = pltpu.make_async_copy(m_rows(k), m_a.at[k], ma_rs.at[k])
    m_in.start()
    send(w_ref, w_all.at[b], w_ss, w_rs, y_pair)

    for o in (4, 3, 5, 2, 6, 1, 7, 0):
        piece = m_a.at[zs[o]]
        arrived(piece, ma_rs.at[zs[o]])
        slot = (8 - o) % 8
        if o:
            send(piece, m_all.at[core, k, slot], mb_ss.at[o], mb_rs.at[slot], line[o])
        else:
            pltpu.make_async_copy(piece, m_all.at[core, k, 0], mb_rs.at[0]).start()

    c_step(1, 0, 1)
    c_step(1, 1, 0)
    c_step(1, 1, 1)

    kh = x * 2 + 1 - h

    def share(piece, n, to_h):
        ref = m_all.at[core, piece]
        if to_h:
            send(ref, ref, m2_ss.at[n], m2_rs.at[core, piece], h_pair)
        for o in (1, 3, 2):
            send(ref, ref, m2_ss.at[n + o], m2_rs.at[core, piece], x_peer[o])

    def to_core(piece, n):
        ref = m_all.at[core, piece]
        send(ref, ref, m3_ss.at[n], m2_rs.at[core, piece], core_pair)

    def got(side, piece):
        arrived(m_all.at[side, piece], m2_rs.at[side, piece])

    def partial(offset):
        for side, dst in ((1 - core, p_send), (core, p_own)):
            total = dot_nt(c_all[offset, 0], w_all[side, 0])
            total += dot_nt(c_all[offset, 1], w_all[side, 1])
            dst[offset] = total.reshape(4, 2, 64, 256)
            if dst is p_send:
                send(p_send.at[offset], p_recv.at[offset], p_ss.at[offset], p_rs.at[offset], core_pair)

    def scatter(offset):
        arrived(p_recv.at[offset], p_rs.at[offset])
        p_own[offset] += p_recv[offset]
        if offset in H_FIRST:
            n = H_FIRST.index(offset)
            send(p_own.at[offset, :, 1 - h], h_recv.at[n], h_ss.at[n], h_rs.at[n], h_pair)
            return
        for o in (2, 1, 3):
            send(
                p_own.at[offset, xs[o]], x_recv.at[offset, o - 1],
                x_ss.at[offset, o - 1], x_rs.at[offset, o - 1], x_peer[o],
            )

    def scatter_more(offset):
        if offset in H_FIRST:
            n = H_FIRST.index(offset)
            arrived(h_recv.at[n], h_rs.at[n])
            h_own[n] = p_own[offset, :, h] + h_recv[n]
            for o in (2, 1, 3):
                send(
                    h_own.at[n, xs[o]], v_recv.at[n, o - 1],
                    v_ss.at[n, o - 1], v_rs.at[n, o - 1], x_peer[o],
                )
            return
        for o in (1, 3, 2):
            arrived(x_recv.at[offset, o - 1], x_rs.at[offset, o - 1])
        total = p_own[offset, x]
        for o in (1, 3, 2):
            total += x_recv[offset, o - 1]
        s_own[offset] = total
        send(s_own.at[offset, 1 - h], y_recv.at[offset], y_ss.at[offset], y_rs.at[offset], h_pair)

    def finish(offset):
        if offset in H_FIRST:
            n = H_FIRST.index(offset)
            for o in (1, 3, 2):
                arrived(v_recv.at[n, o - 1], v_rs.at[n, o - 1])
            total = h_own[n, x]
            for o in (1, 3, 2):
                total += v_recv[n, o - 1]
        else:
            arrived(y_recv.at[offset], y_rs.at[offset])
            total = s_own[offset, h] + y_recv[offset]
        o_send[offset] = total.astype(jnp.bfloat16)

    finals = {}

    def deliver(offset):
        copy = pltpu.make_async_remote_copy(
            src_ref=o_send.at[offset], dst_ref=mg_ref.at[k], send_sem=o_ss.at[offset], recv_sem=o_rs.at[k],
            device_id=home[offset], device_id_type=MESH,
        )
        if offset == 0:
            own = pltpu.make_async_copy(o_send.at[0], mg_ref.at[k], o_rs.at[k])
            pl.when(at_home)(own.start)
            pl.when(jnp.logical_not(at_home))(copy.start)
        else:
            copy.start()
        finals[offset] = copy

    def weight(l, side, offset):
        m_t = m_all[side, :, offset].reshape(512, 256).T
        term = jnp.dot(m_t, c_all[offset, l], preferred_element_type=F32)
        if offset == 0:
            acc[l, side] = term
        else:
            acc[l, side] += term

    def weight_send(l, piece):
        rows = pl.ds(piece * 64, 64)
        send(acc.at[l, 1 - b, rows, :], wg_recv.at[l, rows, :], g_ss.at[l, piece], g_rs.at[l, piece], y_pair)

    def weight_end(l):
        for piece in range(4):
            rows = pl.ds(piece * 64, 64)
            arrived(wg_recv.at[l, rows, :], g_rs.at[l, piece])
            wg_ref[l, rows, :] = acc[l, b, rows, :] + wg_recv[l, rows, :]

    def weights(l, offsets):
        for side in (1 - b, b):
            for o in offsets:
                weight(l, side, o)

    drained = [0]

    def drain(upto):
        for copy in sent[drained[0]:upto]:
            copy.wait_send()
        drained[0] = upto

    def weights(l, offsets):
        for side in (1 - b, b):
            for o in offsets:
                weight(l, side, o)

    drained = [0]

    def drain(upto):
        for copy in sent[drained[0]:upto]:
            copy.wait_send()
        drained[0] = upto

    w_in.wait()
    c_in.wait()
    c_next(1, 0)
    arrived(w_all.at[1 - b], w_rs)
    partial(0)
    for o in range(8):
        arrived(m_all.at[core, k, o], mb_rs.at[o])
    share(k, 0, True)
    to_core(k, 0)
    scatter(0)
    got(core, kh)
    share(kh, 4, False)
    to_core(kh, 1)
    c_next(1, 1)
    partial(7)
    partial(1)
    scatter(7)
    scatter(1)
    c_next(2, 0)
    n = 2
    for o in (1, 3, 2):
        got(core, xs[o] * 2 + h)
        to_core(xs[o] * 2 + h, n)
        n += 1
    scatter_more(0)
    c_next(2, 1, False)
    early = len(sent)
    partial(6)
    partial(2)
    for o in (1, 3, 2):
        got(core, xs[o] * 2 + 1 - h)
        to_core(xs[o] * 2 + 1 - h, n)
        n += 1
    scatter(6)
    scatter(2)
    finish(0)
    scatter_more(1)
    for t in range(8):
        got(1 - core, t)
    weights(0, (0, 7, 1, 6, 2))
    weights(1, (0, 7, 1, 6, 2))
    c_next(3, 0)
    c_step(3, 1, 0)
    c_step(3, 1, 1)
    scatter_more(7)
    weights(0, (5, 3))
    scatter_more(6)
    scatter_more(2)
    drain(early)
    c_next(4, 0)
    weight(0, 1 - b, 4)
    for piece in range(4):
        weight_send(0, piece)
    weight(0, b, 4)
    for o in (7, 1, 6, 2):
        finish(o)
    early = len(sent)
    c_next(3, 1)
    for o in (0, 7, 1, 6, 2):
        deliver(o)
    partial(3)
    partial(5)
    scatter(3)
    scatter(5)
    weights(1, (5, 3))
    drain(early)
    weight_end(0)
    c_next(4, 1)
    partial(4)
    weight(1, 1 - b, 4)
    weight_send(1, 0)
    weight_send(1, 1)
    scatter(4)
    weight(1, b, 4)
    scatter_more(5)
    scatter_more(3)
    weight_send(1, 2)
    scatter_more(4)
    weight_send(1, 3)
    for o in (5, 3, 4):
        finish(o)
        deliver(o)
    weight_end(1)
    for t in range(8):
        arrived(mg_ref.at[t], o_rs.at[t])
    drain(len(sent))
    pl.when(jnp.logical_not(at_home))(finals[0].wait_send)
    for o in range(1, 8):
        finals[o].wait_send()


def on_device(memory, joined_weight, joined_cotangent):
    dma = pltpu.SemaphoreType.DMA
    bf16 = jnp.bfloat16
    memory_grad, weight_grad = pl.pallas_call(
        kernel,
        out_shape=(
            jax.ShapeDtypeStruct((8, 64, 256), bf16),
            jax.ShapeDtypeStruct((2, 256, 512), F32),
        ),
        in_specs=[pl.BlockSpec(memory_space=pltpu.HBM)] * 3,
        out_specs=(pl.BlockSpec(memory_space=pltpu.VMEM),) * 2,
        scratch_shapes=[
            pltpu.VMEM((8, 2, 512, 512), bf16),
            pltpu.VMEM((2, 2, 256, 512), bf16),
            pltpu.VMEM((8, 64, 256), bf16),
            pltpu.VMEM((2, 8, 8, 64, 256), bf16),
            pltpu.VMEM((8, 4, 2, 64, 256), F32),
            pltpu.VMEM((8, 4, 2, 64, 256), F32),
            pltpu.VMEM((8, 4, 2, 64, 256), F32),
            pltpu.VMEM((8, 3, 2, 64, 256), F32),
            pltpu.VMEM((8, 2, 64, 256), F32),
            pltpu.VMEM((8, 64, 256), F32),
            pltpu.VMEM((3, 4, 64, 256), F32),
            pltpu.VMEM((3, 4, 64, 256), F32),
            pltpu.VMEM((3, 3, 64, 256), F32),
            pltpu.VMEM((8, 64, 256), bf16),
            pltpu.VMEM((2, 2, 256, 512), F32),
            pltpu.VMEM((2, 256, 512), F32),
            dma((2,)),
            dma((2, 4, 2, 2)), dma((2, 4, 2, 2)),
            dma, dma,
            dma((8,)), dma((8,)),
            dma((8,)), dma((8,)),
            dma((8,)), dma((2, 8)), dma((8,)),
            dma((8,)), dma((8,)),
            dma((8, 3)), dma((8, 3)),
            dma((8,)), dma((8,)),
            dma((3,)), dma((3,)),
            dma((3, 3)), dma((3, 3)),
            dma((8,)), dma((8,)),
            dma((2, 4)), dma((2, 4)),
        ],
        compiler_params=pltpu.CompilerParams(
            collective_id=0, has_side_effects=True, vmem_limit_bytes=56 * 1024 * 1024
        ),
    )(memory, joined_weight, joined_cotangent)
    return memory_grad.reshape(512, 256), weight_grad


def solution(mesh):
    in_specs = (P("row", "col"), P(None, "row", "col"), P(None, "row", "col"))
    out_specs = (P("row", "col"), P(None, "row", "col"))
    return jax.shard_map(
        on_device, mesh=mesh, in_specs=in_specs, out_specs=out_specs, check_vma=False
    )
```

```python
import jax
import jax.numpy as jnp
from jax import lax
from jax.experimental import pallas as pl
from jax.experimental.pallas import tpu as pltpu
from jax.sharding import PartitionSpec as P

MESH = pl.DeviceIdType.MESH
F32 = jnp.float32
H_FIRST = (1, 2, 3)


def dot_nt(a, b):
    return lax.dot_general(a, b, (((1,), (1,)), ((), ())), preferred_element_type=F32)


def kernel(
    m_ref, w_ref, c_ref, mg_ref, wg_ref, wg_sum, wg_s,
    c_all, w_all, m_a, m_all, p_own, p_send, p_recv, x_recv, s_own, y_recv, h_recv, h_own, v_recv,
    o_send, acc, wg_recv,
    in_s, c_ss, c_rs, w_ss, w_rs, ma_ss, ma_rs, mb_ss, mb_rs, m2_ss, m2_rs, m3_ss, p_ss, p_rs,
    x_ss, x_rs, y_ss, y_rs, h_ss, h_rs, v_ss, v_rs, o_ss, o_rs, g_ss, g_rs,
):
    row, col = lax.axis_index("row"), lax.axis_index("col")
    z, b = lax.div(row, 2), lax.rem(row, 2)
    k, core = lax.div(col, 2), lax.rem(col, 2)
    x, h = lax.div(k, 2), lax.rem(k, 2)
    ks = [lax.rem(k + o, 8) for o in range(8)]
    zs = [lax.rem(z + o, 8) for o in range(8)]
    xs = [lax.rem(x + o, 4) for o in range(4)]
    plane = [(row, ks[o] * 2 + core) for o in range(8)]
    line = [(zs[o] * 2 + b, col) for o in range(8)]
    up, down = line[1], line[7]
    y_pair = (z * 2 + 1 - b, col)
    core_pair = (row, k * 2 + 1 - core)
    h_pair = (row, (x * 2 + 1 - h) * 2 + core)
    x_peer = [(row, (xs[o] * 2 + h) * 2 + core) for o in range(4)]
    home = [(zs[o] * 2 + b, z * 2 + core) for o in range(8)]
    at_home = z == k

    c_in = pltpu.make_async_copy(c_ref, c_all.at[0], in_s.at[0])
    w_in = pltpu.make_async_copy(w_ref, w_all.at[b], in_s.at[1])
    c_in.start()
    w_in.start()

    barrier = pltpu.get_barrier_semaphore()
    greeted = plane[1:] + line[1:] + [y_pair, core_pair]
    for peer in greeted:
        pl.semaphore_signal(barrier, inc=1, device_id=peer, device_id_type=MESH)
    pl.semaphore_wait(barrier, len(greeted))

    sent = []

    def send(src, dst, ss, rs, peer):
        copy = pltpu.make_async_remote_copy(
            src_ref=src, dst_ref=dst, send_sem=ss, recv_sem=rs, device_id=peer, device_id_type=MESH
        )
        copy.start()
        sent.append(copy)

    def arrived(dst, rs):
        pltpu.make_async_copy(dst, dst, rs).wait()

    def part(offset, l, r):
        return c_all.at[offset, l, pl.ds(r * 2, 2)]

    def c_step(step, l, r):
        mine = c_ref.at[l, pl.ds(r * 2, 2)]
        if step < 4 or r == 0:
            src = mine if step == 1 else part(9 - step, l, r)
            send(src, part(8 - step, l, r), c_ss.at[0, step - 1, l, r], c_rs.at[0, step - 1, l, r], up)
        if step < 4 or r == 1:
            src = mine if step == 1 else part(step - 1, l, r)
            send(src, part(step, l, r), c_ss.at[1, step - 1, l, r], c_rs.at[1, step - 1, l, r], down)

    def c_wait(step, l, r):
        if step < 4 or r == 0:
            arrived(part(8 - step, l, r), c_rs.at[0, step - 1, l, r])
        if step < 4 or r == 1:
            arrived(part(step, l, r), c_rs.at[1, step - 1, l, r])

    def c_next(step, l, onward=True):
        for r in range(2):
            c_wait(step, l, r)
            if step < 4 and onward:
                c_step(step + 1, l, r)

    def batch(offset, t, f):
        return c_all.at[offset, 1, :, :, t, :, pl.ds(f * 256, 256)]

    def third_send(t, f):
        g = 1 - f
        send(batch(6, t, f), batch(5, t, f), c_ss.at[0, 2, 1, 2 * t + f], c_rs.at[0, 2, 1, 2 * t + f], up)
        send(batch(2, t, g), batch(3, t, g), c_ss.at[1, 2, 1, 2 * t + g], c_rs.at[1, 2, 1, 2 * t + g], down)

    def third_wait(t, f):
        g = 1 - f
        arrived(batch(5, t, f), c_rs.at[0, 2, 1, 2 * t + f])
        arrived(batch(3, t, g), c_rs.at[1, 2, 1, 2 * t + g])

    def fourth_send(t):
        send(batch(5, t, 0), batch(4, t, 0), c_ss.at[0, 3, 1, t], c_rs.at[0, 3, 1, t], up)
        send(batch(3, t, 1), batch(4, t, 1), c_ss.at[1, 3, 1, t], c_rs.at[1, 3, 1, t], down)

    def fourth_wait(t):
        arrived(batch(4, t, 0), c_rs.at[0, 3, 1, t])
        arrived(batch(4, t, 1), c_rs.at[1, 3, 1, t])

    c_step(1, 0, 0)

    def m_rows(j):
        return m_ref.at[pl.ds(pl.multiple_of(j * 64, 64), 64), :]

    for o in range(1, 8):
        send(m_rows(ks[o]), m_a.at[k], ma_ss.at[o], ma_rs.at[k], plane[o])
    m_in = pltpu.make_async_copy(m_rows(k), m_a.at[k], ma_rs.at[k])
    m_in.start()
    send(w_ref, w_all.at[b], w_ss, w_rs, y_pair)

    for o in (4, 3, 5, 2, 6, 1, 7, 0):
        piece = m_a.at[zs[o]]
        arrived(piece, ma_rs.at[zs[o]])
        slot = (8 - o) % 8
        if o:
            send(piece, m_all.at[core, k, slot], mb_ss.at[o], mb_rs.at[slot], line[o])
        else:
            pltpu.make_async_copy(piece, m_all.at[core, k, 0], mb_rs.at[0]).start()

    c_step(1, 0, 1)
    c_step(1, 1, 0)
    c_step(1, 1, 1)

    kh = x * 2 + 1 - h

    def share(piece, n, to_h):
        ref = m_all.at[core, piece]
        if to_h:
            send(ref, ref, m2_ss.at[n], m2_rs.at[core, piece], h_pair)
        for o in (1, 3, 2):
            send(ref, ref, m2_ss.at[n + o], m2_rs.at[core, piece], x_peer[o])

    def to_core(piece, n):
        ref = m_all.at[core, piece]
        send(ref, ref, m3_ss.at[n], m2_rs.at[core, piece], core_pair)

    def got(side, piece):
        arrived(m_all.at[side, piece], m2_rs.at[side, piece])

    def rows_of(t):
        return slice(None) if t is None else t

    def partial(offset, t=None):
        at, n = rows_of(t), t or 0
        for side, dst in ((1 - core, p_send), (core, p_own)):
            total = dot_nt(c_all[offset, 0, :, :, at].reshape(-1, 512), w_all[side, 0])
            total += dot_nt(c_all[offset, 1, :, :, at].reshape(-1, 512), w_all[side, 1])
            shape = (4, 2, 2, 32, 256) if t is None else (4, 2, 32, 256)
            dst[offset, :, :, at] = total.reshape(shape)
            if dst is p_send:
                send(
                    p_send.at[offset, :, :, at], p_recv.at[offset, :, :, at],
                    p_ss.at[offset, n], p_rs.at[offset, n], core_pair,
                )

    def scatter(offset, t=None):
        at, n = rows_of(t), t or 0
        arrived(p_recv.at[offset, :, :, at], p_rs.at[offset, n])
        p_own[offset, :, :, at] += p_recv[offset, :, :, at]
        if offset in H_FIRST:
            i = H_FIRST.index(offset)
            send(p_own.at[offset, :, 1 - h, at], h_recv.at[i, :, at], h_ss.at[i, n], h_rs.at[i, n], h_pair)
            return
        for o in (2, 1, 3):
            send(
                p_own.at[offset, xs[o], :, at], x_recv.at[offset, o - 1, :, at],
                x_ss.at[offset, o - 1, n], x_rs.at[offset, o - 1, n], x_peer[o],
            )

    def scatter_more(offset, t=None):
        at, n = rows_of(t), t or 0
        if offset in H_FIRST:
            i = H_FIRST.index(offset)
            arrived(h_recv.at[i, :, at], h_rs.at[i, n])
            h_own[i, :, at] = p_own[offset, :, h, at] + h_recv[i, :, at]
            for o in (2, 1, 3):
                send(
                    h_own.at[i, xs[o], at], v_recv.at[i, o - 1, at],
                    v_ss.at[i, o - 1, n], v_rs.at[i, o - 1, n], x_peer[o],
                )
            return
        for o in (1, 3, 2):
            arrived(x_recv.at[offset, o - 1, :, at], x_rs.at[offset, o - 1, n])
        total = p_own[offset, x, :, at]
        for o in (1, 3, 2):
            total += x_recv[offset, o - 1, :, at]
        s_own[offset, :, at] = total
        send(s_own.at[offset, 1 - h, at], y_recv.at[offset, at], y_ss.at[offset, n], y_rs.at[offset, n], h_pair)

    def finish(offset, t=None):
        at, n = rows_of(t), t or 0
        if offset in H_FIRST:
            i = H_FIRST.index(offset)
            for o in (1, 3, 2):
                arrived(v_recv.at[i, o - 1, at], v_rs.at[i, o - 1, n])
            total = h_own[i, x, at]
            for o in (1, 3, 2):
                total += v_recv[i, o - 1, at]
        else:
            arrived(y_recv.at[offset, at], y_rs.at[offset, n])
            total = s_own[offset, h, at] + y_recv[offset, at]
        o_send[offset, at] = total.astype(jnp.bfloat16)

    finals = {}

    def deliver(offset, t=None):
        at, n = rows_of(t), t or 0
        src, dst, rs = o_send.at[offset, at], mg_ref.at[k, at], o_rs.at[k, n]
        copy = pltpu.make_async_remote_copy(
            src_ref=src, dst_ref=dst, send_sem=o_ss.at[offset, n], recv_sem=rs,
            device_id=home[offset], device_id_type=MESH,
        )
        if offset == 0:
            own = pltpu.make_async_copy(src, dst, rs)
            pl.when(at_home)(own.start)
            pl.when(jnp.logical_not(at_home))(copy.start)
        else:
            copy.start()
        finals[offset, n] = copy

    def weight(l, side, offset):
        m_t = m_all[side, :, offset].reshape(512, 256).T
        term = jnp.dot(m_t, c_all[offset, l].reshape(512, 512), preferred_element_type=F32)
        if offset == 0:
            acc[l, side] = term
        else:
            acc[l, side] += term

    def weight_send(l, piece):
        rows = pl.ds(piece * 64, 64)
        send(acc.at[l, 1 - b, rows, :], wg_recv.at[l, rows, :], g_ss.at[l, piece], g_rs.at[l, piece], y_pair)

    results = []

    def weight_end(l):
        for piece in range(4):
            rows = pl.ds(piece * 64, 64)
            arrived(wg_recv.at[l, rows, :], g_rs.at[l, piece])
            wg_sum[l, rows, :] = acc[l, b, rows, :] + wg_recv[l, rows, :]
            copy = pltpu.make_async_copy(wg_sum.at[l, rows, :], wg_ref.at[l, rows, :], wg_s.at[l, piece])
            copy.start()
            results.append(copy)

    def weights(l, offsets):
        for side in (1 - b, b):
            for o in offsets:
                weight(l, side, o)

    drained = [0]

    def drain(upto):
        for copy in sent[drained[0]:upto]:
            copy.wait_send()
        drained[0] = upto

    def weights(l, offsets):
        for side in (1 - b, b):
            for o in offsets:
                weight(l, side, o)

    drained = [0]

    def drain(upto):
        for copy in sent[drained[0]:upto]:
            copy.wait_send()
        drained[0] = upto

    w_in.wait()
    c_in.wait()
    c_next(1, 0)
    arrived(w_all.at[1 - b], w_rs)
    partial(0)
    for o in range(8):
        arrived(m_all.at[core, k, o], mb_rs.at[o])
    share(k, 0, True)
    to_core(k, 0)
    scatter(0)
    got(core, kh)
    share(kh, 4, False)
    to_core(kh, 1)
    c_next(1, 1)
    partial(7)
    partial(1)
    scatter(7)
    scatter(1)
    c_next(2, 0)
    n = 2
    for o in (1, 3, 2):
        got(core, xs[o] * 2 + h)
        to_core(xs[o] * 2 + h, n)
        n += 1
    scatter_more(0)
    c_next(2, 1, False)
    early = len(sent)
    partial(6)
    partial(2)
    for o in (1, 3, 2):
        got(core, xs[o] * 2 + 1 - h)
        to_core(xs[o] * 2 + 1 - h, n)
        n += 1
    scatter(6)
    scatter(2)
    finish(0)
    scatter_more(1)
    for t in range(8):
        got(1 - core, t)
    weights(0, (0, 7, 1, 6, 2))
    weights(1, (0, 7, 1, 6, 2))
    c_next(3, 0)
    third_send(0, 0)
    third_send(0, 1)
    third_send(1, 0)
    scatter_more(7)
    weights(0, (5, 3))
    scatter_more(6)
    scatter_more(2)
    drain(early)
    c_next(4, 0)
    weight(0, 1 - b, 4)
    for piece in range(4):
        weight_send(0, piece)
    weight(0, b, 4)
    third_wait(0, 0)
    fourth_send(0)
    third_send(1, 1)
    for o in (7, 1, 6, 2):
        finish(o)
    third_wait(0, 1)
    partial(3, 0)
    partial(5, 0)
    scatter(3, 0)
    scatter(5, 0)
    early = len(sent)
    third_wait(1, 0)
    fourth_send(1)
    for o in (0, 7, 1, 6, 2):
        deliver(o)
    fourth_wait(0)
    partial(4, 0)
    scatter_more(3, 0)
    scatter_more(5, 0)
    scatter(4, 0)
    drain(early)
    third_wait(1, 1)
    partial(3, 1)
    partial(5, 1)
    weights(1, (5, 3))
    scatter(3, 1)
    scatter(5, 1)
    weight_end(0)
    fourth_wait(1)
    partial(4, 1)
    weight(1, 1 - b, 4)
    weight_send(1, 0)
    weight_send(1, 1)
    scatter(4, 1)
    weight(1, b, 4)
    finish(3, 0)
    deliver(3, 0)
    finish(5, 0)
    deliver(5, 0)
    scatter_more(4, 0)
    scatter_more(5, 1)
    scatter_more(3, 1)
    scatter_more(4, 1)
    weight_send(1, 2)
    weight_send(1, 3)
    for o, t in ((4, 0), (5, 1), (3, 1), (4, 1)):
        finish(o, t)
        deliver(o, t)
    weight_end(1)
    far = z - k
    batched = jnp.logical_or(jnp.abs(far) == 4, jnp.logical_or(jnp.abs(far) == 3, jnp.abs(far) == 5))
    for j in range(8):

        @pl.when(batched)
        def _():
            for t in range(2):
                arrived(mg_ref.at[j, t], o_rs.at[j, t])

        @pl.when(jnp.logical_not(batched))
        def _():
            arrived(mg_ref.at[j], o_rs.at[j, 0])

    for copy in results:
        copy.wait()
    drain(len(sent))
    pl.when(jnp.logical_not(at_home))(finals[0, 0].wait_send)
    for key, copy in finals.items():
        if key[0]:
            copy.wait_send()


def place_kernel(mg_ref, wg_ref, mg_out, wg_out, mg_held, wg_held, sem):
    parts = [(mg_ref, mg_held, mg_out, pl.ds(0, 512))]
    parts += [(wg_ref, wg_held, wg_out, (i // 4, pl.ds(i % 4 * 64, 64))) for i in range(8)]
    loads = [pltpu.make_async_copy(a.at[p], c.at[p], sem.at[0, i]) for i, (a, c, _, p) in enumerate(parts)]
    stores = [pltpu.make_async_copy(c.at[p], d.at[p], sem.at[1, i]) for i, (_, c, d, p) in enumerate(parts)]
    for load in loads:
        load.start()
    for load, store in zip(loads, stores):
        load.wait()
        store.start()
    for store in stores:
        store.wait()


def place(memory_grad, weight_grad):
    return pl.pallas_call(
        place_kernel,
        out_shape=(
            jax.ShapeDtypeStruct((512, 256), jnp.bfloat16),
            jax.ShapeDtypeStruct((2, 256, 512), F32),
        ),
        in_specs=[pl.BlockSpec(memory_space=pltpu.HBM)] * 2,
        out_specs=(pl.BlockSpec(memory_space=pltpu.HBM),) * 2,
        scratch_shapes=[
            pltpu.VMEM((512, 256), jnp.bfloat16),
            pltpu.VMEM((2, 256, 512), F32),
            pltpu.SemaphoreType.DMA((2, 9)),
        ],
    )(memory_grad, weight_grad)


def on_device(memory, joined_weight, joined_cotangent):
    dma = pltpu.SemaphoreType.DMA
    bf16 = jnp.bfloat16
    memory_grad, weight_grad = pl.pallas_call(
        kernel,
        out_shape=(
            jax.ShapeDtypeStruct((8, 2, 32, 256), bf16),
            jax.ShapeDtypeStruct((2, 256, 512), F32),
        ),
        in_specs=[pl.BlockSpec(memory_space=pltpu.HBM)] * 3,
        out_specs=(pl.BlockSpec(memory_space=pltpu.HBM),) * 2,
        scratch_shapes=[
            pltpu.VMEM((2, 256, 512), F32),
            dma((2, 4)),
            pltpu.VMEM((8, 2, 4, 2, 2, 32, 512), bf16),
            pltpu.VMEM((2, 2, 256, 512), bf16),
            pltpu.VMEM((8, 64, 256), bf16),
            pltpu.VMEM((2, 8, 8, 64, 256), bf16),
            pltpu.VMEM((8, 4, 2, 2, 32, 256), F32),
            pltpu.VMEM((8, 4, 2, 2, 32, 256), F32),
            pltpu.VMEM((8, 4, 2, 2, 32, 256), F32),
            pltpu.VMEM((8, 3, 2, 2, 32, 256), F32),
            pltpu.VMEM((8, 2, 2, 32, 256), F32),
            pltpu.VMEM((8, 2, 32, 256), F32),
            pltpu.VMEM((3, 4, 2, 32, 256), F32),
            pltpu.VMEM((3, 4, 2, 32, 256), F32),
            pltpu.VMEM((3, 3, 2, 32, 256), F32),
            pltpu.VMEM((8, 2, 32, 256), bf16),
            pltpu.VMEM((2, 2, 256, 512), F32),
            pltpu.VMEM((2, 256, 512), F32),
            dma((2,)),
            dma((2, 4, 2, 4)), dma((2, 4, 2, 4)),
            dma, dma,
            dma((8,)), dma((8,)),
            dma((8,)), dma((8,)),
            dma((8,)), dma((2, 8)), dma((8,)),
            dma((8, 2)), dma((8, 2)),
            dma((8, 3, 2)), dma((8, 3, 2)),
            dma((8, 2)), dma((8, 2)),
            dma((3, 2)), dma((3, 2)),
            dma((3, 3, 2)), dma((3, 3, 2)),
            dma((8, 2)), dma((8, 2)),
            dma((2, 4)), dma((2, 4)),
        ],
        compiler_params=pltpu.CompilerParams(
            collective_id=0, has_side_effects=True, vmem_limit_bytes=56 * 1024 * 1024
        ),
    )(memory, joined_weight, joined_cotangent.reshape(2, 4, 2, 2, 32, 512))
    return place(memory_grad.reshape(512, 256), weight_grad)


def solution(mesh):
    in_specs = (P("row", "col"), P(None, "row", "col"), P(None, "row", "col"))
    out_specs = (P("row", "col"), P(None, "row", "col"))
    return jax.shard_map(
        on_device, mesh=mesh, in_specs=in_specs, out_specs=out_specs, check_vma=False
    )
```

```python
import jax
import jax.numpy as jnp
from jax import lax
from jax.experimental import pallas as pl
from jax.experimental.pallas import tpu as pltpu
from jax.sharding import PartitionSpec as P

MESH = pl.DeviceIdType.MESH
F32 = jnp.float32
H_FIRST = (1, 2, 3)


def dot_nt(a, b):
    return lax.dot_general(a, b, (((1,), (1,)), ((), ())), preferred_element_type=F32)


def kernel(
    m_ref, w_ref, c_ref, mg_ref, wg_ref, wg_sum, wg_s,
    c_all, w_all, m_a, m_all, p_own, p_send, p_recv, x_recv, s_own, y_recv, h_recv, h_own, v_recv,
    o_send, acc, wg_recv,
    in_s, c_ss, c_rs, w_ss, w_rs, ma_ss, ma_rs, mb_ss, mb_rs, m2_ss, m2_rs, m3_ss, p_ss, p_rs,
    x_ss, x_rs, y_ss, y_rs, h_ss, h_rs, v_ss, v_rs, o_ss, o_rs, g_ss, g_rs,
):
    row, col = lax.axis_index("row"), lax.axis_index("col")
    z, b = lax.div(row, 2), lax.rem(row, 2)
    k, core = lax.div(col, 2), lax.rem(col, 2)
    x, h = lax.div(k, 2), lax.rem(k, 2)
    ks = [lax.rem(k + o, 8) for o in range(8)]
    zs = [lax.rem(z + o, 8) for o in range(8)]
    xs = [lax.rem(x + o, 4) for o in range(4)]
    plane = [(row, ks[o] * 2 + core) for o in range(8)]
    line = [(zs[o] * 2 + b, col) for o in range(8)]
    up, down = line[1], line[7]
    y_pair = (z * 2 + 1 - b, col)
    core_pair = (row, k * 2 + 1 - core)
    h_pair = (row, (x * 2 + 1 - h) * 2 + core)
    x_peer = [(row, (xs[o] * 2 + h) * 2 + core) for o in range(4)]
    home = [(zs[o] * 2 + b, z * 2 + core) for o in range(8)]
    at_home = z == k

    c_in = pltpu.make_async_copy(c_ref, c_all.at[0], in_s.at[0])
    w_in = pltpu.make_async_copy(w_ref, w_all.at[b], in_s.at[1])
    barrier = pltpu.get_barrier_semaphore()
    greeted = plane[1:] + line[1:] + [y_pair, core_pair]
    for peer in greeted:
        pl.semaphore_signal(barrier, inc=1, device_id=peer, device_id_type=MESH)
    pl.semaphore_wait(barrier, len(greeted))

    sent = []

    def send(src, dst, ss, rs, peer):
        copy = pltpu.make_async_remote_copy(
            src_ref=src, dst_ref=dst, send_sem=ss, recv_sem=rs, device_id=peer, device_id_type=MESH
        )
        copy.start()
        sent.append(copy)

    def arrived(dst, rs):
        pltpu.make_async_copy(dst, dst, rs).wait()

    def part(offset, l, r):
        return c_all.at[offset, l, pl.ds(r * 2, 2)]

    def c_step(step, l, r):
        mine = c_ref.at[l, pl.ds(r * 2, 2)]
        if step < 4 or r == 0:
            src = mine if step == 1 else part(9 - step, l, r)
            send(src, part(8 - step, l, r), c_ss.at[0, step - 1, l, r], c_rs.at[0, step - 1, l, r], up)
        if step < 4 or r == 1:
            src = mine if step == 1 else part(step - 1, l, r)
            send(src, part(step, l, r), c_ss.at[1, step - 1, l, r], c_rs.at[1, step - 1, l, r], down)

    def c_wait(step, l, r):
        if step < 4 or r == 0:
            arrived(part(8 - step, l, r), c_rs.at[0, step - 1, l, r])
        if step < 4 or r == 1:
            arrived(part(step, l, r), c_rs.at[1, step - 1, l, r])

    def c_next(step, l, onward=True):
        for r in range(2):
            c_wait(step, l, r)
            if step < 4 and onward:
                c_step(step + 1, l, r)

    def batch(offset, t, f):
        return c_all.at[offset, 1, :, :, t, :, pl.ds(f * 256, 256)]

    def third_send(t, f):
        g = 1 - f
        send(batch(6, t, f), batch(5, t, f), c_ss.at[0, 2, 1, 2 * t + f], c_rs.at[0, 2, 1, 2 * t + f], up)
        send(batch(2, t, g), batch(3, t, g), c_ss.at[1, 2, 1, 2 * t + g], c_rs.at[1, 2, 1, 2 * t + g], down)

    def third_wait(t, f):
        g = 1 - f
        arrived(batch(5, t, f), c_rs.at[0, 2, 1, 2 * t + f])
        arrived(batch(3, t, g), c_rs.at[1, 2, 1, 2 * t + g])

    def fourth_send(t):
        send(batch(5, t, 0), batch(4, t, 0), c_ss.at[0, 3, 1, t], c_rs.at[0, 3, 1, t], up)
        send(batch(3, t, 1), batch(4, t, 1), c_ss.at[1, 3, 1, t], c_rs.at[1, 3, 1, t], down)

    def fourth_wait(t):
        arrived(batch(4, t, 0), c_rs.at[0, 3, 1, t])
        arrived(batch(4, t, 1), c_rs.at[1, 3, 1, t])

    c_step(1, 0, 0)

    def m_rows(j):
        return m_ref.at[pl.ds(pl.multiple_of(j * 64, 64), 64), :]

    for o in range(1, 8):
        send(m_rows(ks[o]), m_a.at[k], ma_ss.at[o], ma_rs.at[k], plane[o])
    m_in = pltpu.make_async_copy(m_rows(k), m_a.at[k], ma_rs.at[k])
    m_in.start()
    send(w_ref, w_all.at[b], w_ss, w_rs, y_pair)
    c_in.start()
    w_in.start()

    for o in (4, 3, 5, 2, 6, 1, 7, 0):
        piece = m_a.at[zs[o]]
        arrived(piece, ma_rs.at[zs[o]])
        slot = (8 - o) % 8
        if o:
            send(piece, m_all.at[core, k, slot], mb_ss.at[o], mb_rs.at[slot], line[o])
        else:
            pltpu.make_async_copy(piece, m_all.at[core, k, 0], mb_rs.at[0]).start()

    c_step(1, 0, 1)
    c_step(1, 1, 0)
    c_step(1, 1, 1)

    kh = x * 2 + 1 - h

    def share(piece, n, to_h):
        ref = m_all.at[core, piece]
        if to_h:
            send(ref, ref, m2_ss.at[n], m2_rs.at[core, piece], h_pair)
        for o in (1, 3, 2):
            send(ref, ref, m2_ss.at[n + o], m2_rs.at[core, piece], x_peer[o])

    def to_core(piece, n):
        ref = m_all.at[core, piece]
        send(ref, ref, m3_ss.at[n], m2_rs.at[core, piece], core_pair)

    def got(side, piece):
        arrived(m_all.at[side, piece], m2_rs.at[side, piece])

    def rows_of(t):
        return slice(None) if t is None else t

    def partial(offset, t=None):
        at, n = rows_of(t), t or 0
        for side, dst in ((1 - core, p_send), (core, p_own)):
            total = dot_nt(c_all[offset, 0, :, :, at].reshape(-1, 512), w_all[side, 0])
            total += dot_nt(c_all[offset, 1, :, :, at].reshape(-1, 512), w_all[side, 1])
            shape = (4, 2, 2, 32, 256) if t is None else (4, 2, 32, 256)
            dst[offset, :, :, at] = total.reshape(shape)
            if dst is p_send:
                send(
                    p_send.at[offset, :, :, at], p_recv.at[offset, :, :, at],
                    p_ss.at[offset, n], p_rs.at[offset, n], core_pair,
                )

    def scatter(offset, t=None):
        at, n = rows_of(t), t or 0
        arrived(p_recv.at[offset, :, :, at], p_rs.at[offset, n])
        p_own[offset, :, :, at] += p_recv[offset, :, :, at]
        if offset in H_FIRST:
            i = H_FIRST.index(offset)
            send(p_own.at[offset, :, 1 - h, at], h_recv.at[i, :, at], h_ss.at[i, n], h_rs.at[i, n], h_pair)
            return
        for o in (2, 1, 3):
            send(
                p_own.at[offset, xs[o], :, at], x_recv.at[offset, o - 1, :, at],
                x_ss.at[offset, o - 1, n], x_rs.at[offset, o - 1, n], x_peer[o],
            )

    def scatter_more(offset, t=None):
        at, n = rows_of(t), t or 0
        if offset in H_FIRST:
            i = H_FIRST.index(offset)
            arrived(h_recv.at[i, :, at], h_rs.at[i, n])
            h_own[i, :, at] = p_own[offset, :, h, at] + h_recv[i, :, at]
            for o in (2, 1, 3):
                send(
                    h_own.at[i, xs[o], at], v_recv.at[i, o - 1, at],
                    v_ss.at[i, o - 1, n], v_rs.at[i, o - 1, n], x_peer[o],
                )
            return
        for o in (1, 3, 2):
            arrived(x_recv.at[offset, o - 1, :, at], x_rs.at[offset, o - 1, n])
        total = p_own[offset, x, :, at]
        for o in (1, 3, 2):
            total += x_recv[offset, o - 1, :, at]
        s_own[offset, :, at] = total
        send(s_own.at[offset, 1 - h, at], y_recv.at[offset, at], y_ss.at[offset, n], y_rs.at[offset, n], h_pair)

    def finish(offset, t=None):
        at, n = rows_of(t), t or 0
        if offset in H_FIRST:
            i = H_FIRST.index(offset)
            for o in (1, 3, 2):
                arrived(v_recv.at[i, o - 1, at], v_rs.at[i, o - 1, n])
            total = h_own[i, x, at]
            for o in (1, 3, 2):
                total += v_recv[i, o - 1, at]
        else:
            arrived(y_recv.at[offset, at], y_rs.at[offset, n])
            total = s_own[offset, h, at] + y_recv[offset, at]
        o_send[offset, at] = total.astype(jnp.bfloat16)

    finals = {}

    def deliver(offset, t=None):
        at, n = rows_of(t), t or 0
        src, dst, rs = o_send.at[offset, at], mg_ref.at[k, at], o_rs.at[k, n]
        copy = pltpu.make_async_remote_copy(
            src_ref=src, dst_ref=dst, send_sem=o_ss.at[offset, n], recv_sem=rs,
            device_id=home[offset], device_id_type=MESH,
        )
        if offset == 0:
            own = pltpu.make_async_copy(src, dst, rs)
            pl.when(at_home)(own.start)
            pl.when(jnp.logical_not(at_home))(copy.start)
        else:
            copy.start()
        finals[offset, n] = copy

    def weight(l, side, offset):
        m_t = m_all[side, :, offset].reshape(512, 256).T
        term = jnp.dot(m_t, c_all[offset, l].reshape(512, 512), preferred_element_type=F32)
        if offset == 0:
            acc[l, side] = term
        else:
            acc[l, side] += term

    def weight_send(l, piece):
        rows = pl.ds(piece * 64, 64)
        send(acc.at[l, 1 - b, rows, :], wg_recv.at[l, rows, :], g_ss.at[l, piece], g_rs.at[l, piece], y_pair)

    results = []

    def weight_end(l):
        for piece in range(4):
            rows = pl.ds(piece * 64, 64)
            arrived(wg_recv.at[l, rows, :], g_rs.at[l, piece])
            wg_sum[l, rows, :] = acc[l, b, rows, :] + wg_recv[l, rows, :]
            copy = pltpu.make_async_copy(wg_sum.at[l, rows, :], wg_ref.at[l, rows, :], wg_s.at[l, piece])
            copy.start()
            results.append(copy)

    def weights(l, offsets):
        for side in (1 - b, b):
            for o in offsets:
                weight(l, side, o)

    drained = [0]

    def drain(upto):
        for copy in sent[drained[0]:upto]:
            copy.wait_send()
        drained[0] = upto

    def weights(l, offsets):
        for side in (1 - b, b):
            for o in offsets:
                weight(l, side, o)

    drained = [0]

    def drain(upto):
        for copy in sent[drained[0]:upto]:
            copy.wait_send()
        drained[0] = upto

    w_in.wait()
    c_in.wait()
    c_next(1, 0)
    arrived(w_all.at[1 - b], w_rs)
    partial(0)
    for o in range(8):
        arrived(m_all.at[core, k, o], mb_rs.at[o])
    share(k, 0, True)
    to_core(k, 0)
    scatter(0)
    got(core, kh)
    share(kh, 4, False)
    to_core(kh, 1)
    c_next(1, 1)
    partial(7)
    partial(1)
    scatter(7)
    scatter(1)
    c_next(2, 0)
    n = 2
    for o in (1, 3, 2):
        got(core, xs[o] * 2 + h)
        to_core(xs[o] * 2 + h, n)
        n += 1
    scatter_more(0)
    c_next(2, 1, False)
    early = len(sent)
    partial(6)
    partial(2)
    for o in (1, 3, 2):
        got(core, xs[o] * 2 + 1 - h)
        to_core(xs[o] * 2 + 1 - h, n)
        n += 1
    scatter(6)
    scatter(2)
    finish(0)
    scatter_more(1)
    for t in range(8):
        got(1 - core, t)
    weights(0, (0, 7, 1, 6, 2))
    weights(1, (0, 7, 1, 6, 2))
    c_next(3, 0)
    third_send(0, 0)
    third_send(0, 1)
    third_send(1, 0)
    scatter_more(7)
    weights(0, (5, 3))
    scatter_more(6)
    scatter_more(2)
    drain(early)
    c_next(4, 0)
    weight(0, 1 - b, 4)
    for piece in range(4):
        weight_send(0, piece)
    weight(0, b, 4)
    third_wait(0, 0)
    fourth_send(0)
    third_send(1, 1)
    for o in (7, 1, 6, 2):
        finish(o)
    third_wait(0, 1)
    partial(3, 0)
    partial(5, 0)
    scatter(3, 0)
    scatter(5, 0)
    early = len(sent)
    third_wait(1, 0)
    fourth_send(1)
    for o in (0, 7, 1, 6, 2):
        deliver(o)
    fourth_wait(0)
    partial(4, 0)
    scatter_more(5, 0)
    scatter(4, 0)
    scatter_more(3, 0)
    drain(early)
    third_wait(1, 1)
    partial(3, 1)
    partial(5, 1)
    weights(1, (5, 3))
    scatter(3, 1)
    scatter(5, 1)
    weight_end(0)
    fourth_wait(1)
    partial(4, 1)
    weight(1, 1 - b, 4)
    weight_send(1, 0)
    weight_send(1, 1)
    scatter(4, 1)
    weight(1, b, 4)
    finish(3, 0)
    deliver(3, 0)
    finish(5, 0)
    deliver(5, 0)
    scatter_more(4, 0)
    scatter_more(5, 1)
    scatter_more(3, 1)
    scatter_more(4, 1)
    weight_send(1, 2)
    weight_send(1, 3)
    for o, t in ((4, 0), (5, 1), (3, 1), (4, 1)):
        finish(o, t)
        deliver(o, t)
    weight_end(1)
    far = z - k
    batched = jnp.logical_or(jnp.abs(far) == 4, jnp.logical_or(jnp.abs(far) == 3, jnp.abs(far) == 5))
    for j in range(8):

        @pl.when(batched)
        def _():
            for t in range(2):
                arrived(mg_ref.at[j, t], o_rs.at[j, t])

        @pl.when(jnp.logical_not(batched))
        def _():
            arrived(mg_ref.at[j], o_rs.at[j, 0])

    for copy in results:
        copy.wait()
    drain(len(sent))
    pl.when(jnp.logical_not(at_home))(finals[0, 0].wait_send)
    for key, copy in finals.items():
        if key[0]:
            copy.wait_send()


def place_kernel(mg_ref, wg_ref, mg_out, wg_out, mg_held, wg_held, sem):
    parts = [(mg_ref, mg_held, mg_out, pl.ds(0, 512))]
    parts += [(wg_ref, wg_held, wg_out, (i // 4, pl.ds(i % 4 * 64, 64))) for i in range(8)]
    loads = [pltpu.make_async_copy(a.at[p], c.at[p], sem.at[0, i]) for i, (a, c, _, p) in enumerate(parts)]
    stores = [pltpu.make_async_copy(c.at[p], d.at[p], sem.at[1, i]) for i, (_, c, d, p) in enumerate(parts)]
    for load in loads:
        load.start()
    for load, store in zip(loads, stores):
        load.wait()
        store.start()
    for store in stores:
        store.wait()


def place(memory_grad, weight_grad):
    return pl.pallas_call(
        place_kernel,
        out_shape=(
            jax.ShapeDtypeStruct((512, 256), jnp.bfloat16),
            jax.ShapeDtypeStruct((2, 256, 512), F32),
        ),
        in_specs=[pl.BlockSpec(memory_space=pltpu.HBM)] * 2,
        out_specs=(pl.BlockSpec(memory_space=pltpu.HBM),) * 2,
        scratch_shapes=[
            pltpu.VMEM((512, 256), jnp.bfloat16),
            pltpu.VMEM((2, 256, 512), F32),
            pltpu.SemaphoreType.DMA((2, 9)),
        ],
    )(memory_grad, weight_grad)


def on_device(memory, joined_weight, joined_cotangent):
    dma = pltpu.SemaphoreType.DMA
    bf16 = jnp.bfloat16
    memory_grad, weight_grad = pl.pallas_call(
        kernel,
        out_shape=(
            jax.ShapeDtypeStruct((8, 2, 32, 256), bf16),
            jax.ShapeDtypeStruct((2, 256, 512), F32),
        ),
        in_specs=[pl.BlockSpec(memory_space=pltpu.HBM)] * 3,
        out_specs=(pl.BlockSpec(memory_space=pltpu.HBM),) * 2,
        scratch_shapes=[
            pltpu.VMEM((2, 256, 512), F32),
            dma((2, 4)),
            pltpu.VMEM((8, 2, 4, 2, 2, 32, 512), bf16),
            pltpu.VMEM((2, 2, 256, 512), bf16),
            pltpu.VMEM((8, 64, 256), bf16),
            pltpu.VMEM((2, 8, 8, 64, 256), bf16),
            pltpu.VMEM((8, 4, 2, 2, 32, 256), F32),
            pltpu.VMEM((8, 4, 2, 2, 32, 256), F32),
            pltpu.VMEM((8, 4, 2, 2, 32, 256), F32),
            pltpu.VMEM((8, 3, 2, 2, 32, 256), F32),
            pltpu.VMEM((8, 2, 2, 32, 256), F32),
            pltpu.VMEM((8, 2, 32, 256), F32),
            pltpu.VMEM((3, 4, 2, 32, 256), F32),
            pltpu.VMEM((3, 4, 2, 32, 256), F32),
            pltpu.VMEM((3, 3, 2, 32, 256), F32),
            pltpu.VMEM((8, 2, 32, 256), bf16),
            pltpu.VMEM((2, 2, 256, 512), F32),
            pltpu.VMEM((2, 256, 512), F32),
            dma((2,)),
            dma((2, 4, 2, 4)), dma((2, 4, 2, 4)),
            dma, dma,
            dma((8,)), dma((8,)),
            dma((8,)), dma((8,)),
            dma((8,)), dma((2, 8)), dma((8,)),
            dma((8, 2)), dma((8, 2)),
            dma((8, 3, 2)), dma((8, 3, 2)),
            dma((8, 2)), dma((8, 2)),
            dma((3, 2)), dma((3, 2)),
            dma((3, 3, 2)), dma((3, 3, 2)),
            dma((8, 2)), dma((8, 2)),
            dma((2, 4)), dma((2, 4)),
        ],
        compiler_params=pltpu.CompilerParams(
            collective_id=0, has_side_effects=True, vmem_limit_bytes=56 * 1024 * 1024
        ),
    )(memory, joined_weight, joined_cotangent.reshape(2, 4, 2, 2, 32, 512))
    return place(memory_grad.reshape(512, 256), weight_grad)


def solution(mesh):
    in_specs = (P("row", "col"), P(None, "row", "col"), P(None, "row", "col"))
    out_specs = (P("row", "col"), P(None, "row", "col"))
    return jax.shard_map(
        on_device, mesh=mesh, in_specs=in_specs, out_specs=out_specs, check_vma=False
    )
```

```python
import jax
import jax.numpy as jnp
from jax import lax
from jax.experimental import pallas as pl
from jax.experimental.pallas import tpu as pltpu
from jax.sharding import PartitionSpec as P

MESH = pl.DeviceIdType.MESH
F32 = jnp.float32
H_FIRST = (1, 2, 3)


def dot_nt(a, b):
    return lax.dot_general(a, b, (((1,), (1,)), ((), ())), preferred_element_type=F32)


def kernel(
    m_ref, w_ref, c_ref, mg_ref, wg_ref, wg_sum, wg_s,
    c_all, w_all, m_a, m_all, p_own, p_send, p_recv, x_recv, s_own, y_recv, h_recv, h_own, v_recv,
    o_send, acc, wg_recv,
    in_s, c_ss, c_rs, w_ss, w_rs, ma_ss, ma_rs, mb_ss, mb_rs, m2_ss, m2_rs, m3_ss, p_ss, p_rs,
    x_ss, x_rs, y_ss, y_rs, h_ss, h_rs, v_ss, v_rs, o_ss, o_rs, g_ss, g_rs,
):
    row, col = lax.axis_index("row"), lax.axis_index("col")
    z, b = lax.div(row, 2), lax.rem(row, 2)
    k, core = lax.div(col, 2), lax.rem(col, 2)
    x, h = lax.div(k, 2), lax.rem(k, 2)
    ks = [lax.rem(k + o, 8) for o in range(8)]
    zs = [lax.rem(z + o, 8) for o in range(8)]
    xs = [lax.rem(x + o, 4) for o in range(4)]
    plane = [(row, ks[o] * 2 + core) for o in range(8)]
    line = [(zs[o] * 2 + b, col) for o in range(8)]
    up, down = line[1], line[7]
    y_pair = (z * 2 + 1 - b, col)
    core_pair = (row, k * 2 + 1 - core)
    h_pair = (row, (x * 2 + 1 - h) * 2 + core)
    x_peer = [(row, (xs[o] * 2 + h) * 2 + core) for o in range(4)]
    home = [(zs[o] * 2 + b, z * 2 + core) for o in range(8)]
    at_home = z == k

    c_in = pltpu.make_async_copy(c_ref, c_all.at[0], in_s.at[0])
    w_in = pltpu.make_async_copy(w_ref, w_all.at[b], in_s.at[1])
    c_in.start()
    w_in.start()

    barrier = pltpu.get_barrier_semaphore()
    greeted = plane[1:] + line[1:] + [y_pair, core_pair]
    for peer in greeted:
        pl.semaphore_signal(barrier, inc=1, device_id=peer, device_id_type=MESH)
    pl.semaphore_wait(barrier, len(greeted))

    sent = []

    def send(src, dst, ss, rs, peer):
        copy = pltpu.make_async_remote_copy(
            src_ref=src, dst_ref=dst, send_sem=ss, recv_sem=rs, device_id=peer, device_id_type=MESH
        )
        copy.start()
        sent.append(copy)

    def arrived(dst, rs):
        pltpu.make_async_copy(dst, dst, rs).wait()

    def part(offset, l, r):
        return c_all.at[offset, l, pl.ds(r * 2, 2)]

    def c_step(step, l, r):
        mine = c_ref.at[l, pl.ds(r * 2, 2)]
        if step < 4 or r == 0:
            src = mine if step == 1 else part(9 - step, l, r)
            send(src, part(8 - step, l, r), c_ss.at[0, step - 1, l, r], c_rs.at[0, step - 1, l, r], up)
        if step < 4 or r == 1:
            src = mine if step == 1 else part(step - 1, l, r)
            send(src, part(step, l, r), c_ss.at[1, step - 1, l, r], c_rs.at[1, step - 1, l, r], down)

    def c_wait(step, l, r):
        if step < 4 or r == 0:
            arrived(part(8 - step, l, r), c_rs.at[0, step - 1, l, r])
        if step < 4 or r == 1:
            arrived(part(step, l, r), c_rs.at[1, step - 1, l, r])

    def c_next(step, l, onward=True):
        for r in range(2):
            c_wait(step, l, r)
            if step < 4 and onward:
                c_step(step + 1, l, r)

    def batch(offset, t, f):
        return c_all.at[offset, 1, :, :, t, :, pl.ds(f * 256, 256)]

    def third_send(t, f):
        g = 1 - f
        send(batch(6, t, f), batch(5, t, f), c_ss.at[0, 2, 1, 2 * t + f], c_rs.at[0, 2, 1, 2 * t + f], up)
        send(batch(2, t, g), batch(3, t, g), c_ss.at[1, 2, 1, 2 * t + g], c_rs.at[1, 2, 1, 2 * t + g], down)

    def third_wait(t, f):
        g = 1 - f
        arrived(batch(5, t, f), c_rs.at[0, 2, 1, 2 * t + f])
        arrived(batch(3, t, g), c_rs.at[1, 2, 1, 2 * t + g])

    def fourth_send(t):
        send(batch(5, t, 0), batch(4, t, 0), c_ss.at[0, 3, 1, t], c_rs.at[0, 3, 1, t], up)
        send(batch(3, t, 1), batch(4, t, 1), c_ss.at[1, 3, 1, t], c_rs.at[1, 3, 1, t], down)

    def fourth_wait(t):
        arrived(batch(4, t, 0), c_rs.at[0, 3, 1, t])
        arrived(batch(4, t, 1), c_rs.at[1, 3, 1, t])

    c_step(1, 0, 0)

    def m_rows(j):
        return m_ref.at[pl.ds(pl.multiple_of(j * 64, 64), 64), :]

    for o in range(1, 8):
        send(m_rows(ks[o]), m_a.at[k], ma_ss.at[o], ma_rs.at[k], plane[o])
    m_in = pltpu.make_async_copy(m_rows(k), m_a.at[k], ma_rs.at[k])
    m_in.start()
    send(w_ref, w_all.at[b], w_ss, w_rs, y_pair)

    for o in (4, 3, 5, 2, 6, 1, 7, 0):
        piece = m_a.at[zs[o]]
        arrived(piece, ma_rs.at[zs[o]])
        slot = (8 - o) % 8
        if o:
            send(piece, m_all.at[core, k, slot], mb_ss.at[o], mb_rs.at[slot], line[o])
        else:
            pltpu.make_async_copy(piece, m_all.at[core, k, 0], mb_rs.at[0]).start()

    c_step(1, 0, 1)
    c_step(1, 1, 0)
    c_step(1, 1, 1)

    kh = x * 2 + 1 - h

    def share(piece, n, to_h):
        ref = m_all.at[core, piece]
        if to_h:
            send(ref, ref, m2_ss.at[n], m2_rs.at[core, piece], h_pair)
        for o in (1, 3, 2):
            send(ref, ref, m2_ss.at[n + o], m2_rs.at[core, piece], x_peer[o])

    def to_core(piece, n):
        ref = m_all.at[core, piece]
        send(ref, ref, m3_ss.at[n], m2_rs.at[core, piece], core_pair)

    def got(side, piece):
        arrived(m_all.at[side, piece], m2_rs.at[side, piece])

    def rows_of(t):
        return slice(None) if t is None else t

    def partial(offset, t=None):
        at, n = rows_of(t), t or 0
        for side, dst in ((1 - core, p_send), (core, p_own)):
            total = dot_nt(c_all[offset, 0, :, :, at].reshape(-1, 512), w_all[side, 0])
            total += dot_nt(c_all[offset, 1, :, :, at].reshape(-1, 512), w_all[side, 1])
            shape = (4, 2, 2, 32, 256) if t is None else (4, 2, 32, 256)
            dst[offset, :, :, at] = total.reshape(shape)
            if dst is p_send:
                send(
                    p_send.at[offset, :, :, at], p_recv.at[offset, :, :, at],
                    p_ss.at[offset, n], p_rs.at[offset, n], core_pair,
                )

    def scatter(offset, t=None):
        at, n = rows_of(t), t or 0
        arrived(p_recv.at[offset, :, :, at], p_rs.at[offset, n])
        p_own[offset, :, :, at] += p_recv[offset, :, :, at]
        if offset in H_FIRST:
            i = H_FIRST.index(offset)
            send(p_own.at[offset, :, 1 - h, at], h_recv.at[i, :, at], h_ss.at[i, n], h_rs.at[i, n], h_pair)
            return
        for o in (2, 1, 3):
            send(
                p_own.at[offset, xs[o], :, at], x_recv.at[offset, o - 1, :, at],
                x_ss.at[offset, o - 1, n], x_rs.at[offset, o - 1, n], x_peer[o],
            )

    def scatter_more(offset, t=None):
        at, n = rows_of(t), t or 0
        if offset in H_FIRST:
            i = H_FIRST.index(offset)
            arrived(h_recv.at[i, :, at], h_rs.at[i, n])
            h_own[i, :, at] = p_own[offset, :, h, at] + h_recv[i, :, at]
            for o in (2, 1, 3):
                send(
                    h_own.at[i, xs[o], at], v_recv.at[i, o - 1, at],
                    v_ss.at[i, o - 1, n], v_rs.at[i, o - 1, n], x_peer[o],
                )
            return
        for o in (1, 3, 2):
            arrived(x_recv.at[offset, o - 1, :, at], x_rs.at[offset, o - 1, n])
        total = p_own[offset, x, :, at]
        for o in (1, 3, 2):
            total += x_recv[offset, o - 1, :, at]
        s_own[offset, :, at] = total
        send(s_own.at[offset, 1 - h, at], y_recv.at[offset, at], y_ss.at[offset, n], y_rs.at[offset, n], h_pair)

    def finish(offset, t=None):
        at, n = rows_of(t), t or 0
        if offset in H_FIRST:
            i = H_FIRST.index(offset)
            for o in (1, 3, 2):
                arrived(v_recv.at[i, o - 1, at], v_rs.at[i, o - 1, n])
            total = h_own[i, x, at]
            for o in (1, 3, 2):
                total += v_recv[i, o - 1, at]
        else:
            arrived(y_recv.at[offset, at], y_rs.at[offset, n])
            total = s_own[offset, h, at] + y_recv[offset, at]
        o_send[offset, at] = total.astype(jnp.bfloat16)

    finals = {}

    def deliver(offset, t=None):
        at, n = rows_of(t), t or 0
        src, dst, rs = o_send.at[offset, at], mg_ref.at[k, at], o_rs.at[k, n]
        copy = pltpu.make_async_remote_copy(
            src_ref=src, dst_ref=dst, send_sem=o_ss.at[offset, n], recv_sem=rs,
            device_id=home[offset], device_id_type=MESH,
        )
        if offset == 0:
            own = pltpu.make_async_copy(src, dst, rs)
            pl.when(at_home)(own.start)
            pl.when(jnp.logical_not(at_home))(copy.start)
        else:
            copy.start()
        finals[offset, n] = copy

    def weight(l, side, offset):
        m_t = m_all[side, :, offset].reshape(512, 256).T
        term = jnp.dot(m_t, c_all[offset, l].reshape(512, 512), preferred_element_type=F32)
        if offset == 0:
            acc[l, side] = term
        else:
            acc[l, side] += term

    def weight_send(l, piece):
        rows = pl.ds(piece * 64, 64)
        send(acc.at[l, 1 - b, rows, :], wg_recv.at[l, rows, :], g_ss.at[l, piece], g_rs.at[l, piece], y_pair)

    results = []

    def weight_end(l):
        for piece in range(4):
            rows = pl.ds(piece * 64, 64)
            arrived(wg_recv.at[l, rows, :], g_rs.at[l, piece])
            wg_sum[l, rows, :] = acc[l, b, rows, :] + wg_recv[l, rows, :]
            copy = pltpu.make_async_copy(wg_sum.at[l, rows, :], wg_ref.at[l, rows, :], wg_s.at[l, piece])
            copy.start()
            results.append(copy)

    def weights(l, offsets):
        for side in (1 - b, b):
            for o in offsets:
                weight(l, side, o)

    drained = [0]

    def drain(upto):
        for copy in sent[drained[0]:upto]:
            copy.wait_send()
        drained[0] = upto

    def weights(l, offsets):
        for side in (1 - b, b):
            for o in offsets:
                weight(l, side, o)

    drained = [0]

    def drain(upto):
        for copy in sent[drained[0]:upto]:
            copy.wait_send()
        drained[0] = upto

    w_in.wait()
    c_in.wait()
    c_next(1, 0)
    arrived(w_all.at[1 - b], w_rs)
    partial(0)
    for o in range(8):
        arrived(m_all.at[core, k, o], mb_rs.at[o])
    share(k, 0, True)
    to_core(k, 0)
    scatter(0)
    got(core, kh)
    share(kh, 4, False)
    to_core(kh, 1)
    c_next(1, 1)
    partial(7)
    partial(1)
    scatter(7)
    scatter(1)
    c_next(2, 0)
    n = 2
    for o in (1, 3, 2):
        got(core, xs[o] * 2 + h)
        to_core(xs[o] * 2 + h, n)
        n += 1
    scatter_more(0)
    c_next(2, 1, False)
    early = len(sent)
    partial(6)
    partial(2)
    for o in (1, 3, 2):
        got(core, xs[o] * 2 + 1 - h)
        to_core(xs[o] * 2 + 1 - h, n)
        n += 1
    scatter(6)
    scatter(2)
    finish(0)
    scatter_more(1)
    for t in range(8):
        got(1 - core, t)
    weights(0, (0, 7, 1, 6, 2))
    weights(1, (0, 7, 1, 6, 2))
    c_next(3, 0)
    third_send(0, 0)
    third_send(0, 1)
    third_send(1, 0)
    scatter_more(7)
    weights(0, (5, 3))
    scatter_more(6)
    scatter_more(2)
    drain(early)
    c_next(4, 0)
    weight(0, 1 - b, 4)
    for piece in range(4):
        weight_send(0, piece)
    weight(0, b, 4)
    third_wait(0, 0)
    fourth_send(0)
    third_send(1, 1)
    for o in (7, 1, 6, 2):
        finish(o)
    third_wait(0, 1)
    partial(3, 0)
    partial(5, 0)
    scatter(3, 0)
    scatter(5, 0)
    early = len(sent)
    third_wait(1, 0)
    fourth_send(1)
    for o in (0, 7, 1, 6, 2):
        deliver(o)
    fourth_wait(0)
    partial(4, 0)
    scatter_more(5, 0)
    scatter(4, 0)
    scatter_more(3, 0)
    drain(early)
    third_wait(1, 1)
    partial(3, 1)
    partial(5, 1)
    weights(1, (5, 3))
    scatter(3, 1)
    scatter(5, 1)
    weight_end(0)
    fourth_wait(1)
    partial(4, 1)
    weight(1, 1 - b, 4)
    weight_send(1, 0)
    weight_send(1, 1)
    scatter(4, 1)
    weight(1, b, 4)
    finish(3, 0)
    deliver(3, 0)
    finish(5, 0)
    deliver(5, 0)
    scatter_more(4, 0)
    scatter_more(5, 1)
    scatter_more(3, 1)
    scatter_more(4, 1)
    weight_send(1, 2)
    weight_send(1, 3)
    for o, t in ((4, 0), (5, 1), (3, 1), (4, 1)):
        finish(o, t)
        deliver(o, t)
    weight_end(1)
    far = z - k
    batched = jnp.logical_or(jnp.abs(far) == 4, jnp.logical_or(jnp.abs(far) == 3, jnp.abs(far) == 5))
    for j in range(8):

        @pl.when(batched)
        def _():
            for t in range(2):
                arrived(mg_ref.at[j, t], o_rs.at[j, t])

        @pl.when(jnp.logical_not(batched))
        def _():
            arrived(mg_ref.at[j], o_rs.at[j, 0])

    for copy in results:
        copy.wait()
    drain(len(sent))
    pl.when(jnp.logical_not(at_home))(finals[0, 0].wait_send)
    for key, copy in finals.items():
        if key[0]:
            copy.wait_send()


def place_kernel(mg_ref, wg_ref, mg_out, wg_out, mg_held, wg_held, sem):
    parts = [(mg_ref, mg_held, mg_out, pl.ds(0, 512))]
    parts += [(wg_ref, wg_held, wg_out, (i // 4, pl.ds(i % 4 * 64, 64))) for i in range(8)]
    loads = [pltpu.make_async_copy(a.at[p], c.at[p], sem.at[0, i]) for i, (a, c, _, p) in enumerate(parts)]
    stores = [pltpu.make_async_copy(c.at[p], d.at[p], sem.at[1, i]) for i, (_, c, d, p) in enumerate(parts)]
    for load in loads:
        load.start()
    for load, store in zip(loads, stores):
        load.wait()
        store.start()
    for store in stores:
        store.wait()


def place(memory_grad, weight_grad):
    return pl.pallas_call(
        place_kernel,
        out_shape=(
            jax.ShapeDtypeStruct((512, 256), jnp.bfloat16),
            jax.ShapeDtypeStruct((2, 256, 512), F32),
        ),
        in_specs=[pl.BlockSpec(memory_space=pltpu.HBM)] * 2,
        out_specs=(pl.BlockSpec(memory_space=pltpu.HBM),) * 2,
        scratch_shapes=[
            pltpu.VMEM((512, 256), jnp.bfloat16),
            pltpu.VMEM((2, 256, 512), F32),
            pltpu.SemaphoreType.DMA((2, 9)),
        ],
    )(memory_grad, weight_grad)


def on_device(memory, joined_weight, joined_cotangent):
    dma = pltpu.SemaphoreType.DMA
    bf16 = jnp.bfloat16
    memory_grad, weight_grad = pl.pallas_call(
        kernel,
        out_shape=(
            jax.ShapeDtypeStruct((8, 2, 32, 256), bf16),
            jax.ShapeDtypeStruct((2, 256, 512), F32),
        ),
        in_specs=[pl.BlockSpec(memory_space=pltpu.HBM)] * 3,
        out_specs=(pl.BlockSpec(memory_space=pltpu.HBM),) * 2,
        scratch_shapes=[
            pltpu.VMEM((2, 256, 512), F32),
            dma((2, 4)),
            pltpu.VMEM((8, 2, 4, 2, 2, 32, 512), bf16),
            pltpu.VMEM((2, 2, 256, 512), bf16),
            pltpu.VMEM((8, 64, 256), bf16),
            pltpu.VMEM((2, 8, 8, 64, 256), bf16),
            pltpu.VMEM((8, 4, 2, 2, 32, 256), F32),
            pltpu.VMEM((8, 4, 2, 2, 32, 256), F32),
            pltpu.VMEM((8, 4, 2, 2, 32, 256), F32),
            pltpu.VMEM((8, 3, 2, 2, 32, 256), F32),
            pltpu.VMEM((8, 2, 2, 32, 256), F32),
            pltpu.VMEM((8, 2, 32, 256), F32),
            pltpu.VMEM((3, 4, 2, 32, 256), F32),
            pltpu.VMEM((3, 4, 2, 32, 256), F32),
            pltpu.VMEM((3, 3, 2, 32, 256), F32),
            pltpu.VMEM((8, 2, 32, 256), bf16),
            pltpu.VMEM((2, 2, 256, 512), F32),
            pltpu.VMEM((2, 256, 512), F32),
            dma((2,)),
            dma((2, 4, 2, 4)), dma((2, 4, 2, 4)),
            dma, dma,
            dma((8,)), dma((8,)),
            dma((8,)), dma((8,)),
            dma((8,)), dma((2, 8)), dma((8,)),
            dma((8, 2)), dma((8, 2)),
            dma((8, 3, 2)), dma((8, 3, 2)),
            dma((8, 2)), dma((8, 2)),
            dma((3, 2)), dma((3, 2)),
            dma((3, 3, 2)), dma((3, 3, 2)),
            dma((8, 2)), dma((8, 2)),
            dma((2, 4)), dma((2, 4)),
        ],
        compiler_params=pltpu.CompilerParams(
            collective_id=0, has_side_effects=True, vmem_limit_bytes=56 * 1024 * 1024
        ),
    )(memory, joined_weight, joined_cotangent.reshape(2, 4, 2, 2, 32, 512))
    return place(memory_grad.reshape(512, 256), weight_grad)


def solution(mesh):
    in_specs = (P("row", "col"), P(None, "row", "col"), P(None, "row", "col"))
    out_specs = (P("row", "col"), P(None, "row", "col"))
    return jax.shard_map(
        on_device, mesh=mesh, in_specs=in_specs, out_specs=out_specs, check_vma=False
    )
```
